32 devices in a mesh: dp: 16 (over z, y, core), tm: 2 (over x).
Axes of the slice: x: 2, y: 2, z: 4, core: 2. Of those that a mesh axis runs over, the one named last changes fastest.
Arguments:
- frames_in: bfloat16 [16, 4, 10, 16, 512], P('dp', 'tm'), may hold values from -6 to 6
- cotangent: bfloat16 [16, 8, 10, 16, 512], P('dp', 'tm'), may hold values from -6 to 6
- w_spatial: bfloat16 [9, 512, 512], P(None, 'dp'), may hold values from -0.09375 to 0.09375
- w_temporal: bfloat16 [3, 512, 512], P(None, 'dp'), may hold values from -0.15625 to 0.15625
Outputs:
- decoded: bfloat16 [16, 8, 10, 16, 512], P('dp', 'tm')
- grad_input: bfloat16 [16, 4, 10, 16, 512], P('dp', 'tm')
- grad_spatial: float32 [9, 512, 512], P(None, 'dp')
- grad_temporal: float32 [3, 512, 512], P(None, 'dp')
The draws below stay inside these ranges and needn't reach their ends.
All inputs are finite; a program needn't handle non-finite values.
Results may differ from the reference program's by a relative error of at most 0.0051.
Values may be sent and summed in bfloat16 or wider, within the bound.
A program may use at most 192 MiB of HBM per device.

```python
import math
import jax
import jax.numpy as jnp
from jax import lax

C = 512
ROWS = 10
COLS = 16
CLIPS = 16
FRAMES = 4
OUT_FRAMES = 8


def level_of(stream_key, extent, pieces, smallest, top_value):
    gain = 1.0
    for dim, shards_of in pieces:
        steps = jax.random.uniform(jax.random.fold_in(jax.random.fold_in(stream_key, 6), dim), (shards_of,), jnp.float32, smallest / len(pieces), top_value / len(pieces))
        gain = gain * jnp.repeat(jnp.exp(steps), extent[dim] // shards_of).reshape((-1,) + (1,) * (len(extent) - 1 - dim))
    return gain


def centred(key, dims, scale, bound, cuts=(), held_as=jnp.bfloat16):
    entries = scale * jax.random.normal(key, dims, jnp.float32)
    if cuts:
        entries = entries * level_of(key, dims, cuts, -0.22, 0.18)
    return jnp.clip(entries, -bound, bound).astype(held_as)


def setup_inputs(seed: int = 0) -> dict:
    streams_of = jax.random.split(jax.random.key(seed), 5)
    frames_in = centred(streams_of[0], (CLIPS, FRAMES, ROWS, COLS, C), 1.0, 6.0, ((0, 16), (1, 2)))
    cotangent = centred(streams_of[1], (CLIPS, OUT_FRAMES, ROWS, COLS, C), 1.0, 6.0, ((0, 16), (1, 2)))
    w_spatial = centred(streams_of[2], (9, C, C), (9 * C) ** -0.5, 0.09375, ((1, 16),))
    w_temporal = centred(streams_of[3], (3, C, C), (3 * C) ** -0.5, 0.15625, ((1, 16),))
    return dict(frames_in=frames_in, cotangent=cotangent, w_spatial=w_spatial, w_temporal=w_temporal)


spatial_taps = [(row_shift, col_shift) for row_shift in range(3) for col_shift in range(3)]

def contract_rows(left, right):
    return lax.dot_general(left, right, (((0,), (0,)), ((), ())), preferred_element_type=jnp.float32)

def contract_cols(left, right):
    return lax.dot_general(left, right, (((1,), (1,)), ((), ())), preferred_element_type=jnp.float32)

def silu_slope(value):
    sigmoid = jax.nn.sigmoid(value)
    return sigmoid * (1.0 + value * (1.0 - sigmoid))

def spatial_forward(padded_act, weight):
    height = padded_act.shape[1] - 2
    width = padded_act.shape[2] - 2
    total = jnp.float32(0.0)
    for position, (row_shift, col_shift) in enumerate(spatial_taps):
        window = padded_act[:, row_shift:row_shift + height, col_shift:col_shift + width].reshape(-1, padded_act.shape[3])
        total = total + jnp.dot(window, weight[position], preferred_element_type=jnp.float32)
    return total

def spatial_transpose(grad_flat, weight, frames, height, width):
    result = jnp.zeros((frames, height + 2, width + 2, weight.shape[1]), jnp.float32)
    for position, (row_shift, col_shift) in enumerate(spatial_taps):
        part = contract_cols(grad_flat, weight[position]).reshape(frames, height, width, weight.shape[1])
        result = result.at[:, row_shift:row_shift + height, col_shift:col_shift + width].add(part)
    return result[:, 1:-1, 1:-1]

def temporal_forward(stacked, weight, frames):
    total = jnp.float32(0.0)
    for lag_step in range(3):
        window = stacked[lag_step:lag_step + frames].reshape(-1, stacked.shape[3])
        total = total + jnp.dot(window, weight[lag_step], preferred_element_type=jnp.float32)
    return total

def temporal_transpose(grad_flat, weight, frames, height, width):
    total = jnp.zeros((frames + 2, height, width, weight.shape[1]), jnp.float32)
    for lag_step in range(3):
        part = contract_cols(grad_flat, weight[lag_step]).reshape(frames, height, width, weight.shape[1])
        total = total + jnp.pad(part, ((lag_step, 2 - lag_step), (0, 0), (0, 0), (0, 0)))
    return total

def clip_pass(source, upstream, w_spatial, w_temporal):
    frames = 2 * source.shape[0]
    height, width, channels = (source.shape[1], source.shape[2], source.shape[3])
    upsampled = jnp.repeat(source, 2, axis=0)
    up_float = upsampled.astype(jnp.float32)
    activated = jax.nn.silu(up_float).astype(jnp.bfloat16)
    padded_act = jnp.pad(activated, ((0, 0), (1, 1), (1, 1), (0, 0)))
    spatial_out = spatial_forward(padded_act, w_spatial).reshape(frames, height, width, channels).astype(jnp.bfloat16)
    stacked = jnp.concatenate([spatial_out[:1], spatial_out[:1], spatial_out], axis=0)
    temporal_sum = temporal_forward(stacked, w_temporal, frames).reshape(frames, height, width, channels)
    decoded = (up_float + temporal_sum).astype(jnp.bfloat16)
    upstream_flat = upstream.reshape(-1, channels)
    pad_grad = temporal_transpose(upstream_flat, w_temporal, frames, height, width)
    inner = pad_grad[2:].at[0].add(pad_grad[0] + pad_grad[1])
    spatial_grad = inner.reshape(-1, channels).astype(jnp.bfloat16)
    grad_temporal = jnp.stack([contract_rows(stacked[lag_step:lag_step + frames].reshape(-1, channels), upstream_flat) for lag_step in range(3)])
    windows = []
    for row_shift, col_shift in spatial_taps:
        window = padded_act[:, row_shift:row_shift + height, col_shift:col_shift + width].reshape(-1, channels)
        windows.append(contract_rows(window, spatial_grad))
    grad_spatial = jnp.stack(windows)
    act_grad = spatial_transpose(spatial_grad, w_spatial, frames, height, width)
    up_grad = upstream.astype(jnp.float32) + act_grad * silu_slope(up_float)
    grad_input = up_grad.reshape(frames // 2, 2, height, width, channels).sum(axis=1).astype(jnp.bfloat16)
    return (decoded, grad_input, grad_spatial, grad_temporal)

def reference(frames_in, cotangent, w_spatial, w_temporal):

    def step(carry, item):
        decoded, grad_input, grad_s, grad_t = clip_pass(item[0], item[1], w_spatial, w_temporal)
        return ((carry[0] + grad_s, carry[1] + grad_t), (decoded, grad_input))
    start_sums = (jnp.zeros((9, C, C), jnp.float32), jnp.zeros((3, C, C), jnp.float32))
    sums, outputs = lax.scan(step, start_sums, (frames_in, cotangent))
    inverse = 1.0 / math.sqrt(CLIPS * OUT_FRAMES * ROWS * COLS)
    return (outputs[0], outputs[1], sums[0] * inverse, sums[1] * inverse)
```

```python
import functools
import math

import jax
import jax.numpy as jnp
from jax import lax
from jax.experimental import pallas as pl
from jax.experimental.pallas import tpu as pltpu
from jax.sharding import PartitionSpec as P

MESH = pl.DeviceIdType.MESH
LINE = 4
PARTS = 4

spatial_taps = [(row_shift, col_shift) for row_shift in range(3) for col_shift in range(3)]


def passed_along(value, axis, steps):
    count = lax.axis_size(axis)
    leading, last = (max(0, -steps), min(count, count - steps))
    return lax.ppermute(value, axis, [(source, source + steps) for source in range(leading, last)])


def contract_rows(left, right):
    return lax.dot_general(
        left, right, (((0,), (0,)), ((), ())), preferred_element_type=jnp.float32
    )


def contract_cols(left, right):
    return lax.dot_general(
        left, right, (((1,), (1,)), ((), ())), preferred_element_type=jnp.float32
    )


def silu_slope(value):
    sigmoid = jax.nn.sigmoid(value)
    return sigmoid * (1.0 + value * (1.0 - sigmoid))


def spatial_forward(padded_act, weight):
    height = padded_act.shape[1] - 2
    width = padded_act.shape[2] - 2
    total = jnp.float32(0.0)
    for position, (row_shift, col_shift) in enumerate(spatial_taps):
        window = padded_act[
            :, row_shift : row_shift + height, col_shift : col_shift + width
        ].reshape(-1, padded_act.shape[3])
        total = total + jnp.dot(window, weight[position], preferred_element_type=jnp.float32)
    return total


def spatial_transpose(grad_flat, weight, frames, height, width):
    result = jnp.zeros((frames, height + 2, width + 2, weight.shape[1]), jnp.float32)
    for position, (row_shift, col_shift) in enumerate(spatial_taps):
        part = contract_cols(grad_flat, weight[position]).reshape(
            frames, height, width, weight.shape[1]
        )
        result = result.at[:, row_shift : row_shift + height, col_shift : col_shift + width].add(
            part
        )
    return result[:, 1:-1, 1:-1]


def temporal_forward(stacked, weight, frames):
    total = jnp.float32(0.0)
    for lag_step in range(3):
        window = stacked[lag_step : lag_step + frames].reshape(-1, stacked.shape[3])
        total = total + jnp.dot(window, weight[lag_step], preferred_element_type=jnp.float32)
    return total


def temporal_transpose(grad_flat, weight, frames, height, width):
    total = jnp.zeros((frames + 2, height, width, weight.shape[1]), jnp.float32)
    for lag_step in range(3):
        part = contract_cols(grad_flat, weight[lag_step]).reshape(
            frames, height, width, weight.shape[1]
        )
        total = total + jnp.pad(part, ((lag_step, 2 - lag_step), (0, 0), (0, 0), (0, 0)))
    return total


def weight_grads(padded_act, stacked, grad_frames, upstream_frames, frames, height, width):
    columns = grad_frames.shape[-1]
    channels = padded_act.shape[-1]
    upstream_flat = upstream_frames.reshape(-1, columns)
    grad_t = jnp.stack(
        [
            contract_rows(
                stacked[lag_step : lag_step + frames].reshape(-1, channels), upstream_flat
            )
            for lag_step in range(3)
        ]
    )
    collected = []
    for row_shift, col_shift in spatial_taps:
        window = padded_act[
            :, row_shift : row_shift + height, col_shift : col_shift + width
        ].reshape(-1, channels)
        collected.append(contract_rows(window, grad_frames))
    return (jnp.stack(collected), grad_t)


def per_device(frames_in, cotangent, w_spatial, w_temporal):
    source = frames_in[0]
    upstream = cotangent[0]
    frames = 2 * source.shape[0]
    height, width, channels = (source.shape[1], source.shape[2], source.shape[3])
    voxels = frames * height * width
    first_device = lax.axis_index("tm") == 0
    upsampled = jnp.repeat(source, 2, axis=0)
    up_float = upsampled.astype(jnp.float32)
    activated = jax.nn.silu(up_float).astype(jnp.bfloat16)
    padded_act = jnp.pad(activated, ((0, 0), (1, 1), (1, 1), (0, 0)))
    columns = padded_act
    spatial_sum = spatial_forward(columns, lax.all_gather(w_spatial, "dp", axis=1, tiled=True))
    spatial_out = spatial_sum.reshape(frames, height, width, channels).astype(jnp.bfloat16)
    previous = passed_along(spatial_out[frames - 2 :], "tm", 1)
    previous = jnp.where(first_device, jnp.broadcast_to(spatial_out[:1], previous.shape), previous)
    stacked = jnp.concatenate([previous, spatial_out], axis=0)
    columns = stacked
    temporal_sum = temporal_forward(
        columns, lax.all_gather(w_temporal, "dp", axis=1, tiled=True), frames
    )
    decoded = (up_float + temporal_sum.reshape(frames, height, width, channels)).astype(
        jnp.bfloat16
    )
    following = passed_along(upstream[:2], "tm", -1)
    extended_flat = jnp.concatenate([upstream, following], axis=0).reshape(-1, channels)
    piece = lax.all_gather(w_temporal, "dp", axis=1, tiled=True)
    pad_grad = temporal_transpose(extended_flat, piece, frames + 2, height, width)
    inner = pad_grad[2 : frames + 2]
    edge = jnp.where(first_device, pad_grad[0] + pad_grad[1], jnp.zeros_like(pad_grad[0]))
    inner = inner.at[0].add(edge)
    inner_grad = inner.reshape(voxels, piece.shape[1])
    spatial_grad = inner_grad.astype(jnp.bfloat16)
    grad_s_local, grad_t_local = weight_grads(
        padded_act, stacked, spatial_grad, upstream, frames, height, width
    )
    owned_s, owned_t = (
        lax.psum_scatter(grad_s_local, "dp", scatter_dimension=1, tiled=True),
        lax.psum_scatter(grad_t_local, "dp", scatter_dimension=1, tiled=True),
    )
    summed_s, summed_t = lax.psum((owned_s, owned_t), "tm")
    piece = lax.all_gather(w_spatial, "dp", axis=1, tiled=True)
    act_flat = spatial_transpose(spatial_grad, piece, frames, height, width).reshape(
        voxels, piece.shape[1]
    )
    act_grad = act_flat.reshape(frames, height, width, channels)
    up_grad = upstream.astype(jnp.float32) + act_grad * silu_slope(up_float)
    grad_input = (
        up_grad.reshape(frames // 2, 2, height, width, channels).sum(axis=1).astype(jnp.bfloat16)
    )
    inverse = 1.0 / math.sqrt(lax.axis_size("dp") * lax.axis_size("tm") * voxels)
    return (decoded[None], grad_input[None], summed_s * inverse, summed_t * inverse)


def places(line, rows):
    index = lax.axis_index("dp")
    core = lax.rem(index, 2)
    row = lax.rem(index // 2, rows)
    return index // (2 * rows), row, core, lax.axis_index("tm")


def block_of(line, row, core, rows):
    return (line * rows + row) * 2 + core


def greet(peers):
    barrier = pltpu.get_barrier_semaphore()
    for peer in peers:
        pl.semaphore_signal(barrier, inc=1, device_id=peer, device_id_type=MESH)
    pl.semaphore_wait(barrier, len(peers))


def peers_of(line, row, core, tm, rows):
    along = [
        (block_of(lax.rem(line + step, LINE), row, core, rows), tm) for step in range(1, LINE)
    ]
    across = [
        (block_of(line, lax.rem(row + step, rows), core, rows), tm) for step in range(1, rows)
    ]
    sibling = (block_of(line, row, 1 - core, rows), tm)
    partner = (block_of(line, row, core, rows), 1 - tm)
    return along, across, sibling, partner


def gather_kernel(
    rows, w_ref, u_ref, c_ref, w_all, u_all, c_all, send_sem, recv_sem, pair_send, pair_recv, own_sem
):
    line, row, core, tm = places(LINE, rows)
    along, across, sibling, partner = peers_of(line, row, core, tm, rows)
    greet(along + across + [sibling, partner])
    taps = w_ref.shape[0] // PARTS
    me = block_of(line, row, core, rows)
    sent = []

    def push(part, source, block, peer, slot):
        copy = pltpu.make_async_remote_copy(
            src_ref=source,
            dst_ref=w_all.at[pl.ds(part * taps, taps), block],
            send_sem=send_sem.at[part, slot],
            recv_sem=recv_sem.at[part, block],
            device_id=peer,
            device_id_type=MESH,
        )
        copy.start()
        sent.append(copy)

    def landed(part, block):
        view = w_all.at[pl.ds(part * taps, taps), block]
        pltpu.make_async_copy(view, view, recv_sem.at[part, block]).wait()
        return view

    first_across = LINE - 1
    first_core = first_across + LINE * (rows - 1)
    for part in range(PARTS):
        own = w_ref.at[pl.ds(part * taps, taps)]
        for step, peer in enumerate(along):
            push(part, own, me, peer, step)
        for step, peer in enumerate(across):
            push(part, own, me, peer, first_across + step)
        push(part, own, me, sibling, first_core)
    pairs = []
    for number, (source, target) in enumerate(((u_ref, u_all), (c_ref, c_all))):
        copy = pltpu.make_async_remote_copy(
            src_ref=source,
            dst_ref=target.at[tm],
            send_sem=pair_send.at[number],
            recv_sem=pair_recv.at[number],
            device_id=partner,
            device_id_type=MESH,
        )
        copy.start()
        pairs.append(copy)
    kept = [
        pltpu.make_async_copy(w_ref, w_all.at[:, me], own_sem.at[0]),
        pltpu.make_async_copy(u_ref, u_all.at[tm], own_sem.at[1]),
        pltpu.make_async_copy(c_ref, c_all.at[tm], own_sem.at[2]),
    ]
    for copy in kept:
        copy.start()

    def relay_line(part):
        for step in range(1, LINE):
            block = block_of(lax.rem(line + step, LINE), row, core, rows)
            view = landed(part, block)
            for number, peer in enumerate(across):
                push(part, view, block, peer, first_across + step * (rows - 1) + number)
            push(part, view, block, sibling, first_core + step)

    def relay_rows(part):
        for number in range(1, rows):
            for step in range(LINE):
                block = block_of(
                    lax.rem(line + step, LINE), lax.rem(row + number, rows), core, rows
                )
                view = landed(part, block)
                push(part, view, block, sibling, first_core + number * LINE + step)

    for part in range(PARTS):
        relay_line(part)
        if part:
            relay_rows(part - 1)
    relay_rows(PARTS - 1)
    for part in range(PARTS):
        for number in range(rows):
            for step in range(LINE):
                landed(part, block_of(step, number, 1 - core, rows))
    for copy in sent:
        copy.wait_send()
    for copy in pairs:
        copy.wait()
    for copy in kept:
        copy.wait()


def gather(weights, source, upstream, devices):
    rows = devices // (2 * LINE)
    slots = (LINE - 1) + LINE * (rows - 1) + LINE * rows
    anywhere = pl.BlockSpec(memory_space=pl.ANY)
    taps, depth, columns = weights.shape
    return pl.pallas_call(
        functools.partial(gather_kernel, rows),
        out_shape=(
            jax.ShapeDtypeStruct((taps, devices, depth, columns), weights.dtype),
            jax.ShapeDtypeStruct((2,) + source.shape, source.dtype),
            jax.ShapeDtypeStruct((2,) + upstream.shape, upstream.dtype),
        ),
        in_specs=[anywhere] * 3,
        out_specs=(anywhere,) * 3,
        scratch_shapes=[
            pltpu.SemaphoreType.DMA((PARTS, slots)),
            pltpu.SemaphoreType.DMA((PARTS, devices)),
            pltpu.SemaphoreType.DMA((2,)),
            pltpu.SemaphoreType.DMA((2,)),
            pltpu.SemaphoreType.DMA((3,)),
        ],
        compiler_params=pltpu.CompilerParams(collective_id=0, has_side_effects=True),
        name="gather_weights",
    )(weights, source, upstream)


def reduce_kernel(
    rows,
    p_ref,
    out_ref,
    from_core,
    to_row,
    from_row,
    to_line,
    from_line,
    core_send,
    core_recv,
    row_send,
    row_recv,
    line_send,
    line_recv,
    pair_send,
    pair_recv,
):
    line, row, core, tm = places(LINE, rows)
    along, across, sibling, partner = peers_of(line, row, core, tm, rows)
    greet(along + across + [sibling, partner])

    def push(source, target, send, recv, peer):
        copy = pltpu.make_async_remote_copy(
            src_ref=source,
            dst_ref=target,
            send_sem=send,
            recv_sem=recv,
            device_id=peer,
            device_id_type=MESH,
        )
        copy.start()
        return copy

    wide = jnp.float32
    sent = []
    order = list(range(1, LINE)) + [0]
    from_sibling = {}
    for number in list(range(1, rows)) + [0]:
        for step in order:
            there = lax.rem(line + step, LINE)
            beside = lax.rem(row + number, rows)
            slot = number * LINE + step
            copy = push(
                p_ref.at[block_of(there, beside, 1 - core, rows)],
                from_core.at[slot],
                core_send.at[slot],
                core_recv.at[slot],
                sibling,
            )
            from_sibling[number, step] = copy
    for number in range(1, rows):
        for step in order:
            there = lax.rem(line + step, LINE)
            beside = lax.rem(row + number, rows)
            slot = number * LINE + step
            from_sibling[number, step].wait_recv()
            to_row[slot] = (
                p_ref[block_of(there, beside, core, rows)].astype(wide)
                + from_core[slot].astype(wide)
            ).astype(jnp.bfloat16)
            sent.append(
                push(
                    to_row.at[slot],
                    from_row.at[slot],
                    row_send.at[slot],
                    row_recv.at[slot],
                    across[number - 1],
                )
            )
    row_copies = {
        (number, step): sent[(number - 1) * LINE + place]
        for number in range(1, rows)
        for place, step in enumerate(order)
    }
    line_copies = []
    for step in order:
        there = lax.rem(line + step, LINE)
        from_sibling[0, step].wait_recv()
        total = p_ref[block_of(there, row, core, rows)].astype(wide) + from_core[step].astype(wide)
        for number in range(1, rows):
            row_copies[number, step].wait_recv()
            total = total + from_row[number * LINE + step].astype(wide)
        if step:
            to_line[step] = total.astype(jnp.bfloat16)
            line_copies.append(
                push(
                    to_line.at[step],
                    from_line.at[step],
                    line_send.at[step],
                    line_recv.at[step],
                    along[step - 1],
                )
            )
        else:
            for copy in line_copies:
                copy.wait_recv()
            for other in range(1, LINE):
                total = total + from_line[other].astype(wide)
            out_ref[tm] = total.astype(jnp.bfloat16)
    last = push(out_ref.at[tm], out_ref.at[tm], pair_send.at[0], pair_recv.at[0], partner)
    for copy in list(from_sibling.values()) + sent + line_copies:
        copy.wait_send()
    last.wait()


def reduce_grads(partial, devices):
    rows = devices // (2 * LINE)
    block = partial.shape[1:]
    in_vmem = pl.BlockSpec(memory_space=pltpu.VMEM)
    many = rows * LINE
    return pl.pallas_call(
        functools.partial(reduce_kernel, rows),
        out_shape=jax.ShapeDtypeStruct((2,) + block, partial.dtype),
        in_specs=[in_vmem],
        out_specs=in_vmem,
        scratch_shapes=[
            pltpu.VMEM((many,) + block, partial.dtype),
            pltpu.VMEM((many,) + block, partial.dtype),
            pltpu.VMEM((many,) + block, partial.dtype),
            pltpu.VMEM((LINE,) + block, partial.dtype),
            pltpu.VMEM((LINE,) + block, partial.dtype),
            pltpu.SemaphoreType.DMA((many,)),
            pltpu.SemaphoreType.DMA((many,)),
            pltpu.SemaphoreType.DMA((many,)),
            pltpu.SemaphoreType.DMA((many,)),
            pltpu.SemaphoreType.DMA((LINE,)),
            pltpu.SemaphoreType.DMA((LINE,)),
            pltpu.SemaphoreType.DMA((1,)),
            pltpu.SemaphoreType.DMA((1,)),
        ],
        compiler_params=pltpu.CompilerParams(
            collective_id=1, has_side_effects=True, vmem_limit_bytes=40 * 2**20
        ),
        name="reduce_grads",
    )(partial)


def beside(frames, direction):
    edges = ((0, 0), (1, 1), (1, 1), (0, 0))
    wide = jnp.pad(frames, edges)
    cols = frames.shape[2]
    shifts = (0, 1, 2) if direction > 0 else (2, 1, 0)
    return jnp.concatenate([wide[:, :, s : s + cols] for s in shifts], axis=-1)


def paired_device(frames_in, cotangent, w_spatial, w_temporal):
    devices = lax.axis_size("dp")
    tm = lax.axis_index("tm")
    source = frames_in[0]
    own, height, width, channels = source.shape
    weights, sources, upstreams = gather(
        jnp.concatenate([w_temporal, w_spatial], axis=0), source, cotangent[0], devices
    )
    weights = weights.reshape(weights.shape[0], channels, channels)
    w_t, w_s = weights[:3], weights[3:]
    clip = sources.reshape((2 * own, height, width, channels))
    upstream = upstreams.reshape((4 * own, height * width, channels))
    frames = 2 * own
    even, odd = upstream[0::2], upstream[1::2]
    nothing = jnp.zeros_like(even[:1])
    even_next = jnp.concatenate([even[1:], nothing], axis=0)
    odd_next = jnp.concatenate([odd[1:], nothing], axis=0)

    def back(frame_list, weight):
        return lax.dot_general(
            frame_list, weight, (((2,), (1,)), ((), ())), preferred_element_type=jnp.float32
        )

    with jax.named_scope("temporal_back"):
        first = (jnp.arange(frames) == 0)[:, None, None]
        grads = (
            back(even, w_t[2])
            + back(odd, w_t[2])
            + back(odd, w_t[1])
            + back(even_next, w_t[1])
            + back(even_next, w_t[0])
            + back(odd_next, w_t[0])
        )
        edge = (
            back(even[:1], w_t[0]) + back(odd[:1], w_t[0]) + back(even[:1], w_t[1])
        )
        grads = jnp.where(first, grads + edge, grads).astype(jnp.bfloat16)

    with jax.named_scope("spatial"):
        activated = jax.nn.silu(clip.astype(jnp.float32)).astype(jnp.bfloat16)
        columns = beside(activated, 1)
        spatial = jnp.float32(0.0)
        for r in range(3):
            spatial = spatial + jnp.dot(
                columns[:, r : r + height].reshape(-1, 3 * channels),
                w_s[3 * r : 3 * r + 3].reshape(3 * channels, channels),
                preferred_element_type=jnp.float32,
            )
        spatial = spatial.astype(jnp.bfloat16).reshape(frames, height * width, channels)
        before = jnp.concatenate([spatial[:1], spatial[:-1]], axis=0)

    with jax.named_scope("weight_grads"):
        half = channels // 2
        start = tm * half
        grads_half = lax.dynamic_slice_in_dim(grads, start, half, 2).reshape(-1, half)
        even_half = lax.dynamic_slice_in_dim(even, start, half, 2).reshape(-1, half)
        odd_half = lax.dynamic_slice_in_dim(odd, start, half, 2).reshape(-1, half)
        both_half = jnp.concatenate([even_half, odd_half], axis=0)
        now, past = spatial.reshape(-1, channels), before.reshape(-1, channels)
        parts = [
            contract_rows(jnp.concatenate([past, past], axis=0), both_half)[None],
            contract_rows(jnp.concatenate([past, now], axis=0), both_half)[None],
            contract_rows(jnp.concatenate([now, now], axis=0), both_half)[None],
        ]
        for r in range(3):
            window = columns[:, r : r + height].reshape(-1, 3 * channels)
            parts.append(contract_rows(window, grads_half).reshape(3, channels, half))
        partial = jnp.concatenate(parts, axis=0).astype(jnp.bfloat16)
        partial = partial.reshape(12, devices, channels // devices, half).transpose(1, 0, 2, 3)
    summed = reduce_grads(partial, devices)

    mine = own * tm
    with jax.named_scope("temporal"):
        now = lax.dynamic_slice_in_dim(spatial, mine, own, 0).reshape(-1, channels)
        past = lax.dynamic_slice_in_dim(before, mine, own, 0).reshape(-1, channels)
        held = source.astype(jnp.float32)
        common = (
            jnp.dot(past, w_t[0], preferred_element_type=jnp.float32)
            + jnp.dot(now, w_t[2], preferred_element_type=jnp.float32)
            + held.reshape(-1, channels)
        )
        ahead = common + jnp.dot(past, w_t[1], preferred_element_type=jnp.float32)
        behind = common + jnp.dot(now, w_t[1], preferred_element_type=jnp.float32)
        decoded = jnp.stack(
            [
                ahead.astype(jnp.bfloat16).reshape(own, height, width, channels),
                behind.astype(jnp.bfloat16).reshape(own, height, width, channels),
            ],
            axis=1,
        ).reshape(2 * own, height, width, channels)
    with jax.named_scope("spatial_back"):
        mine_grads = lax.dynamic_slice_in_dim(grads, mine, own, 0).reshape(
            own, height, width, channels
        )
        spread = beside(mine_grads, -1)
        act_grad = jnp.float32(0.0)
        for r in range(3):
            window = spread[:, 2 - r : 2 - r + height].reshape(-1, 3, channels)
            act_grad = act_grad + lax.dot_general(
                window,
                w_s[3 * r : 3 * r + 3],
                (((1, 2), (0, 2)), ((), ())),
                preferred_element_type=jnp.float32,
            )
        act_grad = act_grad.reshape(own, height, width, channels)
        pair = cotangent[0].reshape(own, 2, height, width, channels).astype(jnp.float32)
        grad_input = (pair[:, 0] + pair[:, 1] + act_grad * silu_slope(held)).astype(jnp.bfloat16)

    inverse = 1.0 / math.sqrt(devices * 2 * frames * height * width)
    whole = jnp.concatenate([summed[0], summed[1]], axis=-1).astype(jnp.float32) * inverse
    return (decoded[None], grad_input[None], whole[3:], whole[:3])


def solution(mesh):
    clip_split = P("dp", "tm", None, None, None)
    rows_split = P(None, "dp", None)
    paired = mesh.shape["tm"] == 2 and mesh.shape["dp"] % (2 * LINE) == 0
    return jax.shard_map(
        paired_device if paired else per_device,
        mesh=mesh,
        in_specs=(clip_split, clip_split, rows_split, rows_split),
        out_specs=(clip_split, clip_split, rows_split, rows_split),
        check_vma=False,
    )
```

```python
import functools
import math

import jax
import jax.numpy as jnp
from jax import lax
from jax.experimental import pallas as pl
from jax.experimental.pallas import tpu as pltpu
from jax.sharding import PartitionSpec as P

MESH = pl.DeviceIdType.MESH
LINE = 4
PARTS = 4

spatial_taps = [(row_shift, col_shift) for row_shift in range(3) for col_shift in range(3)]


def passed_along(value, axis, steps):
    count = lax.axis_size(axis)
    leading, last = (max(0, -steps), min(count, count - steps))
    return lax.ppermute(value, axis, [(source, source + steps) for source in range(leading, last)])


def contract_rows(left, right):
    return lax.dot_general(
        left, right, (((0,), (0,)), ((), ())), preferred_element_type=jnp.float32
    )


def contract_cols(left, right):
    return lax.dot_general(
        left, right, (((1,), (1,)), ((), ())), preferred_element_type=jnp.float32
    )


def silu_slope(value):
    sigmoid = jax.nn.sigmoid(value)
    return sigmoid * (1.0 + value * (1.0 - sigmoid))


def spatial_forward(padded_act, weight):
    height = padded_act.shape[1] - 2
    width = padded_act.shape[2] - 2
    total = jnp.float32(0.0)
    for position, (row_shift, col_shift) in enumerate(spatial_taps):
        window = padded_act[
            :, row_shift : row_shift + height, col_shift : col_shift + width
        ].reshape(-1, padded_act.shape[3])
        total = total + jnp.dot(window, weight[position], preferred_element_type=jnp.float32)
    return total


def spatial_transpose(grad_flat, weight, frames, height, width):
    result = jnp.zeros((frames, height + 2, width + 2, weight.shape[1]), jnp.float32)
    for position, (row_shift, col_shift) in enumerate(spatial_taps):
        part = contract_cols(grad_flat, weight[position]).reshape(
            frames, height, width, weight.shape[1]
        )
        result = result.at[:, row_shift : row_shift + height, col_shift : col_shift + width].add(
            part
        )
    return result[:, 1:-1, 1:-1]


def temporal_forward(stacked, weight, frames):
    total = jnp.float32(0.0)
    for lag_step in range(3):
        window = stacked[lag_step : lag_step + frames].reshape(-1, stacked.shape[3])
        total = total + jnp.dot(window, weight[lag_step], preferred_element_type=jnp.float32)
    return total


def temporal_transpose(grad_flat, weight, frames, height, width):
    total = jnp.zeros((frames + 2, height, width, weight.shape[1]), jnp.float32)
    for lag_step in range(3):
        part = contract_cols(grad_flat, weight[lag_step]).reshape(
            frames, height, width, weight.shape[1]
        )
        total = total + jnp.pad(part, ((lag_step, 2 - lag_step), (0, 0), (0, 0), (0, 0)))
    return total


def weight_grads(padded_act, stacked, grad_frames, upstream_frames, frames, height, width):
    columns = grad_frames.shape[-1]
    channels = padded_act.shape[-1]
    upstream_flat = upstream_frames.reshape(-1, columns)
    grad_t = jnp.stack(
        [
            contract_rows(
                stacked[lag_step : lag_step + frames].reshape(-1, channels), upstream_flat
            )
            for lag_step in range(3)
        ]
    )
    collected = []
    for row_shift, col_shift in spatial_taps:
        window = padded_act[
            :, row_shift : row_shift + height, col_shift : col_shift + width
        ].reshape(-1, channels)
        collected.append(contract_rows(window, grad_frames))
    return (jnp.stack(collected), grad_t)


def per_device(frames_in, cotangent, w_spatial, w_temporal):
    source = frames_in[0]
    upstream = cotangent[0]
    frames = 2 * source.shape[0]
    height, width, channels = (source.shape[1], source.shape[2], source.shape[3])
    voxels = frames * height * width
    first_device = lax.axis_index("tm") == 0
    upsampled = jnp.repeat(source, 2, axis=0)
    up_float = upsampled.astype(jnp.float32)
    activated = jax.nn.silu(up_float).astype(jnp.bfloat16)
    padded_act = jnp.pad(activated, ((0, 0), (1, 1), (1, 1), (0, 0)))
    columns = padded_act
    spatial_sum = spatial_forward(columns, lax.all_gather(w_spatial, "dp", axis=1, tiled=True))
    spatial_out = spatial_sum.reshape(frames, height, width, channels).astype(jnp.bfloat16)
    previous = passed_along(spatial_out[frames - 2 :], "tm", 1)
    previous = jnp.where(first_device, jnp.broadcast_to(spatial_out[:1], previous.shape), previous)
    stacked = jnp.concatenate([previous, spatial_out], axis=0)
    columns = stacked
    temporal_sum = temporal_forward(
        columns, lax.all_gather(w_temporal, "dp", axis=1, tiled=True), frames
    )
    decoded = (up_float + temporal_sum.reshape(frames, height, width, channels)).astype(
        jnp.bfloat16
    )
    following = passed_along(upstream[:2], "tm", -1)
    extended_flat = jnp.concatenate([upstream, following], axis=0).reshape(-1, channels)
    piece = lax.all_gather(w_temporal, "dp", axis=1, tiled=True)
    pad_grad = temporal_transpose(extended_flat, piece, frames + 2, height, width)
    inner = pad_grad[2 : frames + 2]
    edge = jnp.where(first_device, pad_grad[0] + pad_grad[1], jnp.zeros_like(pad_grad[0]))
    inner = inner.at[0].add(edge)
    inner_grad = inner.reshape(voxels, piece.shape[1])
    spatial_grad = inner_grad.astype(jnp.bfloat16)
    grad_s_local, grad_t_local = weight_grads(
        padded_act, stacked, spatial_grad, upstream, frames, height, width
    )
    owned_s, owned_t = (
        lax.psum_scatter(grad_s_local, "dp", scatter_dimension=1, tiled=True),
        lax.psum_scatter(grad_t_local, "dp", scatter_dimension=1, tiled=True),
    )
    summed_s, summed_t = lax.psum((owned_s, owned_t), "tm")
    piece = lax.all_gather(w_spatial, "dp", axis=1, tiled=True)
    act_flat = spatial_transpose(spatial_grad, piece, frames, height, width).reshape(
        voxels, piece.shape[1]
    )
    act_grad = act_flat.reshape(frames, height, width, channels)
    up_grad = upstream.astype(jnp.float32) + act_grad * silu_slope(up_float)
    grad_input = (
        up_grad.reshape(frames // 2, 2, height, width, channels).sum(axis=1).astype(jnp.bfloat16)
    )
    inverse = 1.0 / math.sqrt(lax.axis_size("dp") * lax.axis_size("tm") * voxels)
    return (decoded[None], grad_input[None], summed_s * inverse, summed_t * inverse)


def places(line, rows):
    index = lax.axis_index("dp")
    core = lax.rem(index, 2)
    row = lax.rem(index // 2, rows)
    return index // (2 * rows), row, core, lax.axis_index("tm")


def block_of(line, row, core, rows):
    return (line * rows + row) * 2 + core


def greet(peers):
    barrier = pltpu.get_barrier_semaphore()
    for peer in peers:
        pl.semaphore_signal(barrier, inc=1, device_id=peer, device_id_type=MESH)
    pl.semaphore_wait(barrier, len(peers))


def peers_of(line, row, core, tm, rows):
    along = [
        (block_of(lax.rem(line + step, LINE), row, core, rows), tm) for step in range(1, LINE)
    ]
    across = [
        (block_of(line, lax.rem(row + step, rows), core, rows), tm) for step in range(1, rows)
    ]
    sibling = (block_of(line, row, 1 - core, rows), tm)
    partner = (block_of(line, row, core, rows), 1 - tm)
    return along, across, sibling, partner


def gather_kernel(
    rows, w_ref, u_ref, c_ref, w_all, u_all, c_all, send_sem, recv_sem, pair_send, pair_recv, own_sem
):
    line, row, core, tm = places(LINE, rows)
    along, across, sibling, partner = peers_of(line, row, core, tm, rows)
    greet(along + across + [sibling, partner])
    taps = w_ref.shape[0] // PARTS
    me = block_of(line, row, core, rows)
    sent = []

    def push(part, source, block, peer, slot):
        copy = pltpu.make_async_remote_copy(
            src_ref=source,
            dst_ref=w_all.at[pl.ds(part * taps, taps), block],
            send_sem=send_sem.at[part, slot],
            recv_sem=recv_sem.at[part, block],
            device_id=peer,
            device_id_type=MESH,
        )
        copy.start()
        sent.append(copy)

    def landed(part, block):
        view = w_all.at[pl.ds(part * taps, taps), block]
        pltpu.make_async_copy(view, view, recv_sem.at[part, block]).wait()
        return view

    first_across = LINE - 1
    first_core = first_across + LINE * (rows - 1)
    for part in range(PARTS):
        own = w_ref.at[pl.ds(part * taps, taps)]
        for step, peer in enumerate(along):
            push(part, own, me, peer, step)
        for step, peer in enumerate(across):
            push(part, own, me, peer, first_across + step)
        push(part, own, me, sibling, first_core)
    pairs = []
    for number, (source, target) in enumerate(((u_ref, u_all), (c_ref, c_all))):
        copy = pltpu.make_async_remote_copy(
            src_ref=source,
            dst_ref=target.at[tm],
            send_sem=pair_send.at[number],
            recv_sem=pair_recv.at[number],
            device_id=partner,
            device_id_type=MESH,
        )
        copy.start()
        pairs.append(copy)
    kept = [
        pltpu.make_async_copy(w_ref, w_all.at[:, me], own_sem.at[0]),
        pltpu.make_async_copy(u_ref, u_all.at[tm], own_sem.at[1]),
        pltpu.make_async_copy(c_ref, c_all.at[tm], own_sem.at[2]),
    ]
    for copy in kept:
        copy.start()

    def relay_line(part):
        for step in range(1, LINE):
            block = block_of(lax.rem(line + step, LINE), row, core, rows)
            view = landed(part, block)
            for number, peer in enumerate(across):
                push(part, view, block, peer, first_across + step * (rows - 1) + number)
            push(part, view, block, sibling, first_core + step)

    def relay_rows(part):
        for number in range(1, rows):
            for step in range(LINE):
                block = block_of(
                    lax.rem(line + step, LINE), lax.rem(row + number, rows), core, rows
                )
                view = landed(part, block)
                push(part, view, block, sibling, first_core + number * LINE + step)

    for part in range(PARTS):
        relay_line(part)
        if part:
            relay_rows(part - 1)
    relay_rows(PARTS - 1)
    for part in range(PARTS):
        for number in range(rows):
            for step in range(LINE):
                landed(part, block_of(step, number, 1 - core, rows))
    for copy in sent:
        copy.wait_send()
    for copy in pairs:
        copy.wait()
    for copy in kept:
        copy.wait()


def gather(weights, source, upstream, devices):
    rows = devices // (2 * LINE)
    slots = (LINE - 1) + LINE * (rows - 1) + LINE * rows
    anywhere = pl.BlockSpec(memory_space=pl.ANY)
    taps, depth, columns = weights.shape
    return pl.pallas_call(
        functools.partial(gather_kernel, rows),
        out_shape=(
            jax.ShapeDtypeStruct((taps, devices, depth, columns), weights.dtype),
            jax.ShapeDtypeStruct((2,) + source.shape, source.dtype),
            jax.ShapeDtypeStruct((2,) + upstream.shape, upstream.dtype),
        ),
        in_specs=[anywhere] * 3,
        out_specs=(anywhere,) * 3,
        scratch_shapes=[
            pltpu.SemaphoreType.DMA((PARTS, slots)),
            pltpu.SemaphoreType.DMA((PARTS, devices)),
            pltpu.SemaphoreType.DMA((2,)),
            pltpu.SemaphoreType.DMA((2,)),
            pltpu.SemaphoreType.DMA((3,)),
        ],
        compiler_params=pltpu.CompilerParams(collective_id=0, has_side_effects=True),
        name="gather_weights",
    )(weights, source, upstream)


def reduce_kernel(
    rows,
    p_ref,
    out_ref,
    from_core,
    to_row,
    from_row,
    to_line,
    from_line,
    core_send,
    core_recv,
    row_send,
    row_recv,
    line_send,
    line_recv,
    pair_send,
    pair_recv,
):
    line, row, core, tm = places(LINE, rows)
    along, across, sibling, partner = peers_of(line, row, core, tm, rows)
    greet(along + across + [sibling, partner])

    def push(source, target, send, recv, peer):
        copy = pltpu.make_async_remote_copy(
            src_ref=source,
            dst_ref=target,
            send_sem=send,
            recv_sem=recv,
            device_id=peer,
            device_id_type=MESH,
        )
        copy.start()
        return copy

    wide = jnp.float32
    sent = []
    order = list(range(1, LINE)) + [0]
    from_sibling = {}
    for number in list(range(1, rows)) + [0]:
        for step in order:
            there = lax.rem(line + step, LINE)
            beside = lax.rem(row + number, rows)
            slot = number * LINE + step
            copy = push(
                p_ref.at[block_of(there, beside, 1 - core, rows)],
                from_core.at[slot],
                core_send.at[slot],
                core_recv.at[slot],
                sibling,
            )
            from_sibling[number, step] = copy
    for number in range(1, rows):
        for step in order:
            there = lax.rem(line + step, LINE)
            beside = lax.rem(row + number, rows)
            slot = number * LINE + step
            from_sibling[number, step].wait_recv()
            to_row[slot] = (
                p_ref[block_of(there, beside, core, rows)].astype(wide)
                + from_core[slot].astype(wide)
            ).astype(jnp.bfloat16)
            sent.append(
                push(
                    to_row.at[slot],
                    from_row.at[slot],
                    row_send.at[slot],
                    row_recv.at[slot],
                    across[number - 1],
                )
            )
    row_copies = {
        (number, step): sent[(number - 1) * LINE + place]
        for number in range(1, rows)
        for place, step in enumerate(order)
    }
    line_copies = []
    for step in order:
        there = lax.rem(line + step, LINE)
        from_sibling[0, step].wait_recv()
        total = p_ref[block_of(there, row, core, rows)].astype(wide) + from_core[step].astype(wide)
        for number in range(1, rows):
            row_copies[number, step].wait_recv()
            total = total + from_row[number * LINE + step].astype(wide)
        if step:
            to_line[step] = total.astype(jnp.bfloat16)
            line_copies.append(
                push(
                    to_line.at[step],
                    from_line.at[step],
                    line_send.at[step],
                    line_recv.at[step],
                    along[step - 1],
                )
            )
        else:
            for copy in line_copies:
                copy.wait_recv()
            for other in range(1, LINE):
                total = total + from_line[other].astype(wide)
            out_ref[tm] = total.astype(jnp.bfloat16)
    last = push(out_ref.at[tm], out_ref.at[tm], pair_send.at[0], pair_recv.at[0], partner)
    for copy in list(from_sibling.values()) + sent + line_copies:
        copy.wait_send()
    last.wait()


def reduce_grads(partial, devices):
    rows = devices // (2 * LINE)
    block = partial.shape[1:]
    in_vmem = pl.BlockSpec(memory_space=pltpu.VMEM)
    many = rows * LINE
    return pl.pallas_call(
        functools.partial(reduce_kernel, rows),
        out_shape=jax.ShapeDtypeStruct((2,) + block, partial.dtype),
        in_specs=[in_vmem],
        out_specs=in_vmem,
        scratch_shapes=[
            pltpu.VMEM((many,) + block, partial.dtype),
            pltpu.VMEM((many,) + block, partial.dtype),
            pltpu.VMEM((many,) + block, partial.dtype),
            pltpu.VMEM((LINE,) + block, partial.dtype),
            pltpu.VMEM((LINE,) + block, partial.dtype),
            pltpu.SemaphoreType.DMA((many,)),
            pltpu.SemaphoreType.DMA((many,)),
            pltpu.SemaphoreType.DMA((many,)),
            pltpu.SemaphoreType.DMA((many,)),
            pltpu.SemaphoreType.DMA((LINE,)),
            pltpu.SemaphoreType.DMA((LINE,)),
            pltpu.SemaphoreType.DMA((1,)),
            pltpu.SemaphoreType.DMA((1,)),
        ],
        compiler_params=pltpu.CompilerParams(
            collective_id=1, has_side_effects=True, vmem_limit_bytes=40 * 2**20
        ),
        name="reduce_grads",
    )(partial)


def wide_dot(left, right):
    return jnp.dot(left, right, preferred_element_type=jnp.float32)


def column_shifts(flat, width):
    count = flat.shape[0]
    column = lax.rem(lax.broadcasted_iota(jnp.int32, flat.shape, 0), width)
    left = jnp.where(column == 0, 0.0, pltpu.roll(flat, 1, 0))
    right = jnp.where(column == width - 1, 0.0, pltpu.roll(flat, count - 1, 0))
    return left, flat, right


def fill_columns(target, place, flat, width, flip):
    channels = flat.shape[1]
    shifts = column_shifts(flat, width)
    for number, value in enumerate(shifts[::-1] if flip else shifts):
        target[place : place + flat.shape[0], number * channels : (number + 1) * channels] = (
            value.astype(jnp.bfloat16)
        )


def finish(tm, width, w_ref, held, upstream, s_ref, g_ref, spread, decoded_ref, input_ref):
    channels = w_ref.shape[2]
    own, _, pixels, _ = decoded_ref.shape
    stride = pixels + width
    start = tm * (own * pixels)
    past = s_ref[pl.ds(pl.multiple_of(start, 16), own * pixels)]
    now = s_ref[pl.ds(pl.multiple_of(start + pixels, 16), own * pixels)]
    base = wide_dot(past, w_ref[0]) + wide_dot(now, w_ref[2])
    ahead = base + wide_dot(past, w_ref[1])
    behind = base + wide_dot(now, w_ref[1])
    for frame in range(own):
        rows = slice(frame * pixels, (frame + 1) * pixels)
        value = held(frame).astype(jnp.float32)
        decoded_ref[frame, 0] = (value + ahead[rows]).astype(jnp.bfloat16)
        decoded_ref[frame, 1] = (value + behind[rows]).astype(jnp.bfloat16)
    spread[...] = jnp.zeros_like(spread)
    for frame in range(own):
        place = 2 * width + (tm * own + frame) * stride
        flat = g_ref[pl.ds(pl.multiple_of(place, 16), pixels)].astype(jnp.float32)
        fill_columns(spread, width + frame * stride, flat, width, True)
    span = own * stride - width
    total = jnp.zeros((span, channels), jnp.float32)
    for r in range(3):
        for s in range(3):
            total = total + contract_cols(
                spread[(2 - r) * width : (2 - r) * width + span, s * channels : (s + 1) * channels],
                w_ref[3 + 3 * r + s],
            )
    for frame in range(own):
        part = total[frame * stride : frame * stride + pixels]
        value = held(frame).astype(jnp.float32)
        pair = upstream(frame).astype(jnp.float32)
        sigmoid = 1.0 / (1.0 + jnp.exp(-value))
        slope = sigmoid * (1.0 + value * (1.0 - sigmoid))
        input_ref[frame] = (pair[0] + pair[1] + part * slope).astype(jnp.bfloat16)


def compute_kernel(
    width,
    tm_ref,
    w_ref,
    u_ref,
    c_ref,
    p_ref,
    decoded_ref,
    input_ref,
    columns,
    columns_t,
    s_ref,
    s_t,
    g_ref,
    even_ref,
    odd_ref,
    spread,
):
    tm = tm_ref[0]
    frames, pixels, channels = u_ref.shape
    stride = pixels + width
    span = frames * stride - width
    half = p_ref.shape[3]
    own = frames // 2
    lanes = pl.ds(pl.multiple_of(tm * half, half), half)

    def store(tap, value):
        p_ref[:, tap] = value.astype(jnp.bfloat16).reshape(p_ref.shape[0], p_ref.shape[2], half)

    for scratch in (columns, s_ref, g_ref, even_ref, odd_ref):
        scratch[...] = jnp.zeros_like(scratch)
    for frame in range(frames):
        value = u_ref[frame].astype(jnp.float32)
        fill_columns(columns, width + frame * stride, value / (1.0 + jnp.exp(-value)), width, False)
        even_ref[(frame + 1) * pixels : (frame + 2) * pixels] = c_ref[frame, 0]
        odd_ref[(frame + 1) * pixels : (frame + 2) * pixels] = c_ref[frame, 1]
    columns_t[...] = columns[...].T

    even = even_ref[pixels : (frames + 1) * pixels]
    odd = odd_ref[pixels : (frames + 1) * pixels]
    here = (
        contract_cols(even, w_ref[2]) + contract_cols(odd, w_ref[2]) + contract_cols(odd, w_ref[1])
    )
    ahead = (
        contract_cols(even, w_ref[0]) + contract_cols(odd, w_ref[0]) + contract_cols(even, w_ref[1])
    )
    for frame in range(frames):
        value = here[frame * pixels : (frame + 1) * pixels]
        if frame == 0:
            value = value + ahead[:pixels]
        if frame < frames - 1:
            value = value + ahead[(frame + 1) * pixels : (frame + 2) * pixels]
        place = 2 * width + frame * stride
        g_ref[place : place + pixels] = value.astype(jnp.bfloat16)

    depth = columns.shape[0]
    for r in range(3):
        begin = (2 - r) * width
        value = wide_dot(columns_t[...], g_ref[begin : begin + depth, lanes])
        for s in range(3):
            store(3 + 3 * r + s, value[s * channels : (s + 1) * channels])

    total = jnp.zeros((span, channels), jnp.float32)
    for r in range(3):
        total = total + wide_dot(
            columns[r * width : r * width + span],
            w_ref[3 + 3 * r : 6 + 3 * r].reshape(3 * channels, channels),
        )
    for frame in range(frames):
        value = total[frame * stride : frame * stride + pixels].astype(jnp.bfloat16)
        s_ref[(frame + 1) * pixels : (frame + 2) * pixels] = value
        if frame == 0:
            s_ref[:pixels] = value
    s_t[...] = s_ref[...].T
    extent = s_ref.shape[0]
    past_even = wide_dot(s_t[...], even_ref[pixels : pixels + extent, lanes])
    now_odd = wide_dot(s_t[...], odd_ref[:extent, lanes])
    store(1, past_even + now_odd)
    store(0, past_even + wide_dot(s_t[...], odd_ref[pixels : pixels + extent, lanes]))
    store(2, now_odd + wide_dot(s_t[...], even_ref[:extent, lanes]))

    finish(
        tm,
        width,
        w_ref,
        lambda frame: u_ref[tm * own + frame],
        lambda frame: c_ref[tm * own + frame],
        s_ref,
        g_ref,
        spread,
        decoded_ref,
        input_ref,
    )


def up_to(count, step):
    return -(-count // step) * step


def compute(tm, weights, clip, upstream, width, devices):
    frames, pixels, channels = clip.shape
    taps, half, own = weights.shape[0], channels // 2, frames // 2
    stride = pixels + width
    depth = up_to(width + frames * stride, 256)
    extent = up_to((frames + 1) * pixels, 128)
    in_vmem = pl.BlockSpec(memory_space=pltpu.VMEM)
    kept = clip.dtype
    return pl.pallas_call(
        functools.partial(compute_kernel, width),
        out_shape=(
            jax.ShapeDtypeStruct((devices, taps, channels // devices, half), kept),
            jax.ShapeDtypeStruct((own, 2, pixels, channels), kept),
            jax.ShapeDtypeStruct((own, pixels, channels), kept),
        ),
        in_specs=[pl.BlockSpec(memory_space=pltpu.SMEM)] + [in_vmem] * 3,
        out_specs=(in_vmem,) * 3,
        scratch_shapes=[
            pltpu.VMEM((depth, 3 * channels), kept),
            pltpu.VMEM((3 * channels, depth), kept),
            pltpu.VMEM((extent, channels), kept),
            pltpu.VMEM((channels, extent), kept),
            pltpu.VMEM((depth + 2 * width, channels), kept),
            pltpu.VMEM((extent + pixels, channels), kept),
            pltpu.VMEM((extent + pixels, channels), kept),
            pltpu.VMEM((width + own * stride, 3 * channels), kept),
        ],
        compiler_params=pltpu.CompilerParams(vmem_limit_bytes=56 * 2**20),
        cost_estimate=pl.CostEstimate(
            flops=20 * frames * pixels * channels * channels * 2,
            bytes_accessed=12 * 2**20,
            transcendentals=2 * frames * pixels * channels,
        ),
        name="convs_and_grads",
    )(tm, weights, clip, upstream)


def paired_device(frames_in, cotangent, w_spatial, w_temporal):
    devices = lax.axis_size("dp")
    tm = lax.axis_index("tm").astype(jnp.int32).reshape(1)
    source = frames_in[0]
    own, height, width, channels = source.shape
    frames, pixels = 2 * own, height * width
    weights, sources, upstreams = gather(
        jnp.concatenate([w_temporal, w_spatial], axis=0),
        source.reshape(own, pixels, channels),
        cotangent[0].reshape(own, 2, pixels, channels),
        devices,
    )
    partial, decoded, grad_input = compute(
        tm,
        weights.reshape(weights.shape[0], channels, channels),
        sources.reshape(frames, pixels, channels),
        upstreams.reshape(frames, 2, pixels, channels),
        width,
        devices,
    )
    summed = reduce_grads(partial, devices)
    inverse = 1.0 / math.sqrt(devices * 2 * frames * pixels)
    whole = jnp.concatenate([summed[0], summed[1]], axis=-1).astype(jnp.float32) * inverse
    return (
        decoded.reshape(1, 2 * own, height, width, channels),
        grad_input.reshape(1, own, height, width, channels),
        whole[3:],
        whole[:3],
    )


def solution(mesh):
    clip_split = P("dp", "tm", None, None, None)
    rows_split = P(None, "dp", None)
    paired = mesh.shape["tm"] == 2 and mesh.shape["dp"] % (2 * LINE) == 0
    return jax.shard_map(
        paired_device if paired else per_device,
        mesh=mesh,
        in_specs=(clip_split, clip_split, rows_split, rows_split),
        out_specs=(clip_split, clip_split, rows_split, rows_split),
        check_vma=False,
    )
```

```python
import functools
import math

import jax
import jax.numpy as jnp
from jax import lax
from jax.experimental import pallas as pl
from jax.experimental.pallas import tpu as pltpu
from jax.sharding import PartitionSpec as P

MESH = pl.DeviceIdType.MESH
LINE = 4
PARTS = 4

spatial_taps = [(row_shift, col_shift) for row_shift in range(3) for col_shift in range(3)]


def passed_along(value, axis, steps):
    count = lax.axis_size(axis)
    leading, last = (max(0, -steps), min(count, count - steps))
    return lax.ppermute(value, axis, [(source, source + steps) for source in range(leading, last)])


def contract_rows(left, right):
    return lax.dot_general(
        left, right, (((0,), (0,)), ((), ())), preferred_element_type=jnp.float32
    )


def contract_cols(left, right):
    return lax.dot_general(
        left, right, (((1,), (1,)), ((), ())), preferred_element_type=jnp.float32
    )


def silu_slope(value):
    sigmoid = jax.nn.sigmoid(value)
    return sigmoid * (1.0 + value * (1.0 - sigmoid))


def spatial_forward(padded_act, weight):
    height = padded_act.shape[1] - 2
    width = padded_act.shape[2] - 2
    total = jnp.float32(0.0)
    for position, (row_shift, col_shift) in enumerate(spatial_taps):
        window = padded_act[
            :, row_shift : row_shift + height, col_shift : col_shift + width
        ].reshape(-1, padded_act.shape[3])
        total = total + jnp.dot(window, weight[position], preferred_element_type=jnp.float32)
    return total


def spatial_transpose(grad_flat, weight, frames, height, width):
    result = jnp.zeros((frames, height + 2, width + 2, weight.shape[1]), jnp.float32)
    for position, (row_shift, col_shift) in enumerate(spatial_taps):
        part = contract_cols(grad_flat, weight[position]).reshape(
            frames, height, width, weight.shape[1]
        )
        result = result.at[:, row_shift : row_shift + height, col_shift : col_shift + width].add(
            part
        )
    return result[:, 1:-1, 1:-1]


def temporal_forward(stacked, weight, frames):
    total = jnp.float32(0.0)
    for lag_step in range(3):
        window = stacked[lag_step : lag_step + frames].reshape(-1, stacked.shape[3])
        total = total + jnp.dot(window, weight[lag_step], preferred_element_type=jnp.float32)
    return total


def temporal_transpose(grad_flat, weight, frames, height, width):
    total = jnp.zeros((frames + 2, height, width, weight.shape[1]), jnp.float32)
    for lag_step in range(3):
        part = contract_cols(grad_flat, weight[lag_step]).reshape(
            frames, height, width, weight.shape[1]
        )
        total = total + jnp.pad(part, ((lag_step, 2 - lag_step), (0, 0), (0, 0), (0, 0)))
    return total


def weight_grads(padded_act, stacked, grad_frames, upstream_frames, frames, height, width):
    columns = grad_frames.shape[-1]
    channels = padded_act.shape[-1]
    upstream_flat = upstream_frames.reshape(-1, columns)
    grad_t = jnp.stack(
        [
            contract_rows(
                stacked[lag_step : lag_step + frames].reshape(-1, channels), upstream_flat
            )
            for lag_step in range(3)
        ]
    )
    collected = []
    for row_shift, col_shift in spatial_taps:
        window = padded_act[
            :, row_shift : row_shift + height, col_shift : col_shift + width
        ].reshape(-1, channels)
        collected.append(contract_rows(window, grad_frames))
    return (jnp.stack(collected), grad_t)


def per_device(frames_in, cotangent, w_spatial, w_temporal):
    source = frames_in[0]
    upstream = cotangent[0]
    frames = 2 * source.shape[0]
    height, width, channels = (source.shape[1], source.shape[2], source.shape[3])
    voxels = frames * height * width
    first_device = lax.axis_index("tm") == 0
    upsampled = jnp.repeat(source, 2, axis=0)
    up_float = upsampled.astype(jnp.float32)
    activated = jax.nn.silu(up_float).astype(jnp.bfloat16)
    padded_act = jnp.pad(activated, ((0, 0), (1, 1), (1, 1), (0, 0)))
    columns = padded_act
    spatial_sum = spatial_forward(columns, lax.all_gather(w_spatial, "dp", axis=1, tiled=True))
    spatial_out = spatial_sum.reshape(frames, height, width, channels).astype(jnp.bfloat16)
    previous = passed_along(spatial_out[frames - 2 :], "tm", 1)
    previous = jnp.where(first_device, jnp.broadcast_to(spatial_out[:1], previous.shape), previous)
    stacked = jnp.concatenate([previous, spatial_out], axis=0)
    columns = stacked
    temporal_sum = temporal_forward(
        columns, lax.all_gather(w_temporal, "dp", axis=1, tiled=True), frames
    )
    decoded = (up_float + temporal_sum.reshape(frames, height, width, channels)).astype(
        jnp.bfloat16
    )
    following = passed_along(upstream[:2], "tm", -1)
    extended_flat = jnp.concatenate([upstream, following], axis=0).reshape(-1, channels)
    piece = lax.all_gather(w_temporal, "dp", axis=1, tiled=True)
    pad_grad = temporal_transpose(extended_flat, piece, frames + 2, height, width)
    inner = pad_grad[2 : frames + 2]
    edge = jnp.where(first_device, pad_grad[0] + pad_grad[1], jnp.zeros_like(pad_grad[0]))
    inner = inner.at[0].add(edge)
    inner_grad = inner.reshape(voxels, piece.shape[1])
    spatial_grad = inner_grad.astype(jnp.bfloat16)
    grad_s_local, grad_t_local = weight_grads(
        padded_act, stacked, spatial_grad, upstream, frames, height, width
    )
    owned_s, owned_t = (
        lax.psum_scatter(grad_s_local, "dp", scatter_dimension=1, tiled=True),
        lax.psum_scatter(grad_t_local, "dp", scatter_dimension=1, tiled=True),
    )
    summed_s, summed_t = lax.psum((owned_s, owned_t), "tm")
    piece = lax.all_gather(w_spatial, "dp", axis=1, tiled=True)
    act_flat = spatial_transpose(spatial_grad, piece, frames, height, width).reshape(
        voxels, piece.shape[1]
    )
    act_grad = act_flat.reshape(frames, height, width, channels)
    up_grad = upstream.astype(jnp.float32) + act_grad * silu_slope(up_float)
    grad_input = (
        up_grad.reshape(frames // 2, 2, height, width, channels).sum(axis=1).astype(jnp.bfloat16)
    )
    inverse = 1.0 / math.sqrt(lax.axis_size("dp") * lax.axis_size("tm") * voxels)
    return (decoded[None], grad_input[None], summed_s * inverse, summed_t * inverse)


def places(line, rows):
    index = lax.axis_index("dp")
    core = lax.rem(index, 2)
    row = lax.rem(index // 2, rows)
    return index // (2 * rows), row, core, lax.axis_index("tm")


def block_of(line, row, core, rows):
    return (line * rows + row) * 2 + core


def greet(peers):
    barrier = pltpu.get_barrier_semaphore()
    for peer in peers:
        pl.semaphore_signal(barrier, inc=1, device_id=peer, device_id_type=MESH)
    pl.semaphore_wait(barrier, len(peers))


def peers_of(line, row, core, tm, rows):
    along = [
        (block_of(lax.rem(line + step, LINE), row, core, rows), tm) for step in range(1, LINE)
    ]
    across = [
        (block_of(line, lax.rem(row + step, rows), core, rows), tm) for step in range(1, rows)
    ]
    sibling = (block_of(line, row, 1 - core, rows), tm)
    partner = (block_of(line, row, core, rows), 1 - tm)
    return along, across, sibling, partner


def wide_dot(left, right):
    return jnp.dot(left, right, preferred_element_type=jnp.float32)


def column_shifts(flat, width):
    count = flat.shape[0]
    column = lax.rem(lax.broadcasted_iota(jnp.int32, flat.shape, 0), width)
    left = jnp.where(column == 0, 0.0, pltpu.roll(flat, 1, 0))
    right = jnp.where(column == width - 1, 0.0, pltpu.roll(flat, count - 1, 0))
    return left, flat, right


def fill_columns(target, place, flat, width, flip):
    channels = flat.shape[1]
    shifts = column_shifts(flat, width)
    for number, value in enumerate(shifts[::-1] if flip else shifts):
        target[place : place + flat.shape[0], number * channels : (number + 1) * channels] = (
            value.astype(jnp.bfloat16)
        )


def up_to(count, step):
    return -(-count // step) * step


def section_kernel(
    rows,
    width,
    w_ref,
    u_ref,
    c_ref,
    decoded_ref,
    input_ref,
    out_ref,
    w_all,
    u_all,
    c_all,
    partial,
    columns,
    columns_t,
    s_ref,
    s_t,
    g_ref,
    even_ref,
    odd_ref,
    spread,
    total_ref,
    from_core,
    to_row,
    from_row,
    to_line,
    from_line,
    send_sem,
    recv_sem,
    pair_send,
    pair_recv,
    own_sem,
    core_send,
    core_recv,
    row_send,
    row_recv,
    line_send,
    line_recv,
    last_send,
    last_recv,
):
    line, row, core, tm = places(LINE, rows)
    along, across, sibling, partner = peers_of(line, row, core, tm, rows)
    greet(along + across + [sibling, partner])
    taps = w_ref.shape[0] // PARTS
    me = block_of(line, row, core, rows)
    own, _, pixels, channels = c_ref.shape
    frames = 2 * own
    stride = pixels + width
    span = frames * stride - width
    half = partial.shape[3]
    lanes = pl.ds(pl.multiple_of(tm * half, half), half)
    wide = jnp.float32
    narrow = jnp.bfloat16
    sent = []

    def remote(source, target, send, recv, peer):
        copy = pltpu.make_async_remote_copy(
            src_ref=source,
            dst_ref=target,
            send_sem=send,
            recv_sem=recv,
            device_id=peer,
            device_id_type=MESH,
        )
        copy.start()
        return copy

    def push(part, source, block, peer, slot):
        target = w_all.at[pl.ds(part * taps, taps), block]
        sent.append(
            remote(source, target, send_sem.at[part, slot], recv_sem.at[part, block], peer)
        )

    def landed(part, block):
        view = w_all.at[pl.ds(part * taps, taps), block]
        pltpu.make_async_copy(view, view, recv_sem.at[part, block]).wait()
        return view

    first_across = LINE - 1
    first_core = first_across + LINE * (rows - 1)

    def push_own(part):
        block = w_ref.at[pl.ds(part * taps, taps)]
        for step, peer in enumerate(along):
            push(part, block, me, peer, step)
        for step, peer in enumerate(across):
            push(part, block, me, peer, first_across + step)
        push(part, block, me, sibling, first_core)

    def relay_line(part):
        for step in range(1, LINE):
            block = block_of(lax.rem(line + step, LINE), row, core, rows)
            view = landed(part, block)
            for number, peer in enumerate(across):
                push(part, view, block, peer, first_across + step * (rows - 1) + number)
            push(part, view, block, sibling, first_core + step)

    def relay_rows(part):
        for number in range(1, rows):
            for step in range(LINE):
                block = block_of(
                    lax.rem(line + step, LINE), lax.rem(row + number, rows), core, rows
                )
                push(part, landed(part, block), block, sibling, first_core + number * LINE + step)

    def complete(part):
        for number in range(rows):
            for step in range(LINE):
                landed(part, block_of(step, number, 1 - core, rows))

    def tap(number):
        return w_all[number].reshape(channels, channels)

    order = list(range(1, LINE)) + [0]
    core_copies, row_copies, line_copies, last_copies = {}, {}, {}, []
    groups = ((3, 9), (0, 3))

    def sum_core(group):
        chosen = pl.ds(*groups[group])
        for number in list(range(1, rows)) + [0]:
            for step in order:
                slot = number * LINE + step
                block = block_of(
                    lax.rem(line + step, LINE), lax.rem(row + number, rows), 1 - core, rows
                )
                core_copies[group, slot] = remote(
                    partial.at[block, chosen],
                    from_core.at[slot, chosen],
                    core_send.at[group, slot],
                    core_recv.at[group, slot],
                    sibling,
                )

    def of_chip(group, number, step):
        chosen = pl.ds(*groups[group])
        slot = number * LINE + step
        block = block_of(lax.rem(line + step, LINE), lax.rem(row + number, rows), core, rows)
        core_copies[group, slot].wait_recv()
        return partial[block, chosen].astype(wide) + from_core[slot, chosen].astype(wide)

    def sum_rows(group):
        chosen = pl.ds(*groups[group])
        for number in range(1, rows):
            for step in order:
                slot = number * LINE + step
                to_row[slot, chosen] = of_chip(group, number, step).astype(narrow)
                row_copies[group, slot] = remote(
                    to_row.at[slot, chosen],
                    from_row.at[slot, chosen],
                    row_send.at[group, slot],
                    row_recv.at[group, slot],
                    across[number - 1],
                )

    def of_rows(group, step):
        value = of_chip(group, 0, step)
        for number in range(1, rows):
            slot = number * LINE + step
            row_copies[group, slot].wait_recv()
            value = value + from_row[slot, pl.ds(*groups[group])].astype(wide)
        return value

    def sum_line(group):
        chosen = pl.ds(*groups[group])
        for step in range(1, LINE):
            to_line[step, chosen] = of_rows(group, step).astype(narrow)
            line_copies[group, step] = remote(
                to_line.at[step, chosen],
                from_line.at[step, chosen],
                line_send.at[group, step],
                line_recv.at[group, step],
                along[step - 1],
            )

    def sum_last(group):
        chosen = pl.ds(*groups[group])
        value = of_rows(group, 0)
        for step in range(1, LINE):
            line_copies[group, step].wait_recv()
            value = value + from_line[step, chosen].astype(wide)
        out_ref[tm, chosen] = value.astype(narrow)
        view = out_ref.at[tm, chosen]
        last_copies.append(
            remote(view, view, last_send.at[group], last_recv.at[group], partner)
        )

    def store(number, value):
        partial[:, number] = value.astype(narrow).reshape(
            partial.shape[0], partial.shape[2], half
        )

    def lay_out():
        for frame in range(frames):
            value = u_all[frame // own, frame % own].astype(wide)
            fill_columns(
                columns, width + frame * stride, value / (1.0 + jnp.exp(-value)), width, False
            )
            place = slice((frame + 1) * pixels, (frame + 2) * pixels)
            even_ref[place] = c_all[frame // own, frame % own, 0]
            odd_ref[place] = c_all[frame // own, frame % own, 1]
        columns_t[...] = columns[...].T

    def temporal_back():
        even = even_ref[pixels : (frames + 1) * pixels]
        odd = odd_ref[pixels : (frames + 1) * pixels]
        here = contract_cols(even, tap(2)) + contract_cols(odd, tap(2))
        here = here + contract_cols(odd, tap(1))
        ahead = contract_cols(even, tap(0)) + contract_cols(odd, tap(0))
        ahead = ahead + contract_cols(even, tap(1))
        for frame in range(frames):
            value = here[frame * pixels : (frame + 1) * pixels]
            if frame == 0:
                value = value + ahead[:pixels]
            if frame < frames - 1:
                value = value + ahead[(frame + 1) * pixels : (frame + 2) * pixels]
            place = 2 * width + frame * stride
            g_ref[place : place + pixels] = value.astype(narrow)

    def spatial_weight_grads():
        depth = columns.shape[0]
        for r in range(3):
            begin = (2 - r) * width
            value = wide_dot(columns_t[...], g_ref[begin : begin + depth, lanes])
            for s in range(3):
                store(3 + 3 * r + s, value[s * channels : (s + 1) * channels])

    def spatial_row(r):
        value = wide_dot(
            columns[r * width : r * width + span],
            w_all[3 + 3 * r : 6 + 3 * r].reshape(3 * channels, channels),
        )
        total_ref[...] = value if r == 0 else total_ref[...] + value

    def spatial_done():
        for frame in range(frames):
            value = total_ref[frame * stride : frame * stride + pixels].astype(narrow)
            s_ref[(frame + 1) * pixels : (frame + 2) * pixels] = value
            if frame == 0:
                s_ref[:pixels] = value

    def temporal_weight_grads():
        s_t[...] = s_ref[...].T
        extent = s_ref.shape[0]
        past_even = wide_dot(s_t[...], even_ref[pixels : pixels + extent, lanes])
        now_odd = wide_dot(s_t[...], odd_ref[:extent, lanes])
        store(1, past_even + now_odd)
        store(0, past_even + wide_dot(s_t[...], odd_ref[pixels : pixels + extent, lanes]))
        store(2, now_odd + wide_dot(s_t[...], even_ref[:extent, lanes]))

    def decode():
        start = tm * (own * pixels)
        past = s_ref[pl.ds(pl.multiple_of(start, 16), own * pixels)]
        now = s_ref[pl.ds(pl.multiple_of(start + pixels, 16), own * pixels)]
        base = wide_dot(past, tap(0)) + wide_dot(now, tap(2))
        first = base + wide_dot(past, tap(1))
        second = base + wide_dot(now, tap(1))
        for frame in range(own):
            place = slice(frame * pixels, (frame + 1) * pixels)
            value = u_all[tm, frame].astype(wide)
            decoded_ref[frame, 0] = (value + first[place]).astype(narrow)
            decoded_ref[frame, 1] = (value + second[place]).astype(narrow)

    def spatial_back():
        for frame in range(own):
            place = 2 * width + (tm * own + frame) * stride
            flat = g_ref[pl.ds(pl.multiple_of(place, 16), pixels)].astype(wide)
            fill_columns(spread, width + frame * stride, flat, width, True)
        count = own * stride - width
        value = jnp.zeros((count, channels), wide)
        for r in range(3):
            begin = (2 - r) * width
            for s in range(3):
                value = value + contract_cols(
                    spread[begin : begin + count, s * channels : (s + 1) * channels],
                    tap(3 + 3 * r + s),
                )
        for frame in range(own):
            part = value[frame * stride : frame * stride + pixels]
            held = u_all[tm, frame].astype(wide)
            sigmoid = 1.0 / (1.0 + jnp.exp(-held))
            slope = sigmoid * (1.0 + held * (1.0 - sigmoid))
            pair = c_all[tm, frame, 0].astype(wide) + c_all[tm, frame, 1].astype(wide)
            input_ref[frame] = (pair + part * slope).astype(narrow)

    push_own(0)
    pairs = [
        remote(u_ref, u_all.at[tm], pair_send.at[0], pair_recv.at[0], partner),
        remote(c_ref, c_all.at[tm], pair_send.at[1], pair_recv.at[1], partner),
    ]
    for part in range(1, PARTS):
        push_own(part)
    kept = [
        pltpu.make_async_copy(w_ref, w_all.at[:, me], own_sem.at[0]),
        pltpu.make_async_copy(u_ref, u_all.at[tm], own_sem.at[1]),
        pltpu.make_async_copy(c_ref, c_all.at[tm], own_sem.at[2]),
    ]
    for copy in kept:
        copy.start()
    for scratch in (columns, s_ref, g_ref, even_ref, odd_ref, spread):
        scratch[...] = jnp.zeros_like(scratch)
    relay_line(0)
    relay_line(1)
    relay_rows(0)
    for copy in kept:
        copy.wait()
    for copy in pairs:
        copy.wait_recv()
    lay_out()
    relay_line(2)
    relay_rows(1)
    complete(0)
    temporal_back()
    relay_line(3)
    relay_rows(2)
    spatial_weight_grads()
    sum_core(0)
    complete(1)
    spatial_row(0)
    relay_rows(3)
    sum_rows(0)
    complete(2)
    spatial_row(1)
    complete(3)
    spatial_row(2)
    spatial_done()
    temporal_weight_grads()
    sum_core(1)
    sum_line(0)
    sum_rows(1)
    decode()
    sum_line(1)
    spatial_back()
    sum_last(0)
    sum_last(1)
    for copy in sent + pairs:
        copy.wait_send()
    for copies in (core_copies, row_copies, line_copies):
        for copy in copies.values():
            copy.wait_send()
    for copy in last_copies:
        copy.wait()


def section(weights, source, upstream, width, devices):
    rows = devices // (2 * LINE)
    own, pixels, channels = source.shape
    taps, block, _ = weights.shape
    frames, half = 2 * own, channels // 2
    stride = pixels + width
    depth = up_to(width + frames * stride, 256)
    extent = up_to((frames + 1) * pixels, 128)
    many = rows * LINE
    slots = (LINE - 1) + LINE * (rows - 1) + many
    kept = source.dtype
    anywhere = pl.BlockSpec(memory_space=pl.ANY)
    in_vmem = pl.BlockSpec(memory_space=pltpu.VMEM)
    dma = pltpu.SemaphoreType.DMA
    return pl.pallas_call(
        functools.partial(section_kernel, rows, width),
        out_shape=(
            jax.ShapeDtypeStruct((own, 2, pixels, channels), kept),
            jax.ShapeDtypeStruct((own, pixels, channels), kept),
            jax.ShapeDtypeStruct((2, taps, block, half), kept),
        ),
        in_specs=[anywhere] * 3,
        out_specs=(in_vmem,) * 3,
        scratch_shapes=[
            pltpu.VMEM((taps, devices, block, channels), kept),
            pltpu.VMEM((2, own, pixels, channels), kept),
            pltpu.VMEM((2, own, 2, pixels, channels), kept),
            pltpu.VMEM((devices, taps, block, half), kept),
            pltpu.VMEM((depth, 3 * channels), kept),
            pltpu.VMEM((3 * channels, depth), kept),
            pltpu.VMEM((extent, channels), kept),
            pltpu.VMEM((channels, extent), kept),
            pltpu.VMEM((depth + 2 * width, channels), kept),
            pltpu.VMEM((extent + pixels, channels), kept),
            pltpu.VMEM((extent + pixels, channels), kept),
            pltpu.VMEM((width + own * stride, 3 * channels), kept),
            pltpu.VMEM((frames * stride - width, channels), jnp.float32),
            pltpu.VMEM((many, taps, block, half), kept),
            pltpu.VMEM((many, taps, block, half), kept),
            pltpu.VMEM((many, taps, block, half), kept),
            pltpu.VMEM((LINE, taps, block, half), kept),
            pltpu.VMEM((LINE, taps, block, half), kept),
            dma((PARTS, slots)),
            dma((PARTS, devices)),
            dma((2,)),
            dma((2,)),
            dma((3,)),
            dma((2, many)),
            dma((2, many)),
            dma((2, many)),
            dma((2, many)),
            dma((2, LINE)),
            dma((2, LINE)),
            dma((2,)),
            dma((2,)),
        ],
        compiler_params=pltpu.CompilerParams(
            collective_id=0, has_side_effects=True, vmem_limit_bytes=58 * 2**20
        ),
        cost_estimate=pl.CostEstimate(
            flops=20 * frames * pixels * channels * channels * 2,
            bytes_accessed=12 * 2**20,
            transcendentals=2 * frames * pixels * channels,
        ),
        name="section",
    )(weights, source, upstream)


def paired_device(frames_in, cotangent, w_spatial, w_temporal):
    devices = lax.axis_size("dp")
    source = frames_in[0]
    own, height, width, channels = source.shape
    frames, pixels = 2 * own, height * width
    decoded, grad_input, summed = section(
        jnp.concatenate([w_temporal, w_spatial], axis=0),
        source.reshape(own, pixels, channels),
        cotangent[0].reshape(own, 2, pixels, channels),
        width,
        devices,
    )
    inverse = 1.0 / math.sqrt(devices * 2 * frames * pixels)
    whole = jnp.concatenate([summed[0], summed[1]], axis=-1).astype(jnp.float32) * inverse
    return (
        decoded.reshape(1, 2 * own, height, width, channels),
        grad_input.reshape(1, own, height, width, channels),
        whole[3:],
        whole[:3],
    )


def solution(mesh):
    clip_split = P("dp", "tm", None, None, None)
    rows_split = P(None, "dp", None)
    paired = mesh.shape["tm"] == 2 and mesh.shape["dp"] % (2 * LINE) == 0
    return jax.shard_map(
        paired_device if paired else per_device,
        mesh=mesh,
        in_specs=(clip_split, clip_split, rows_split, rows_split),
        out_specs=(clip_split, clip_split, rows_split, rows_split),
        check_vma=False,
    )
```

```python
import functools
import math

import jax
import jax.numpy as jnp
from jax import lax
from jax.experimental import pallas as pl
from jax.experimental.pallas import tpu as pltpu
from jax.sharding import PartitionSpec as P

MESH = pl.DeviceIdType.MESH
LINE = 4
PARTS = 4

spatial_taps = [(row_shift, col_shift) for row_shift in range(3) for col_shift in range(3)]


def passed_along(value, axis, steps):
    count = lax.axis_size(axis)
    leading, last = (max(0, -steps), min(count, count - steps))
    return lax.ppermute(value, axis, [(source, source + steps) for source in range(leading, last)])


def contract_rows(left, right):
    return lax.dot_general(
        left, right, (((0,), (0,)), ((), ())), preferred_element_type=jnp.float32
    )


def contract_cols(left, right):
    return lax.dot_general(
        left, right, (((1,), (1,)), ((), ())), preferred_element_type=jnp.float32
    )


def silu_slope(value):
    sigmoid = jax.nn.sigmoid(value)
    return sigmoid * (1.0 + value * (1.0 - sigmoid))


def spatial_forward(padded_act, weight):
    height = padded_act.shape[1] - 2
    width = padded_act.shape[2] - 2
    total = jnp.float32(0.0)
    for position, (row_shift, col_shift) in enumerate(spatial_taps):
        window = padded_act[
            :, row_shift : row_shift + height, col_shift : col_shift + width
        ].reshape(-1, padded_act.shape[3])
        total = total + jnp.dot(window, weight[position], preferred_element_type=jnp.float32)
    return total


def spatial_transpose(grad_flat, weight, frames, height, width):
    result = jnp.zeros((frames, height + 2, width + 2, weight.shape[1]), jnp.float32)
    for position, (row_shift, col_shift) in enumerate(spatial_taps):
        part = contract_cols(grad_flat, weight[position]).reshape(
            frames, height, width, weight.shape[1]
        )
        result = result.at[:, row_shift : row_shift + height, col_shift : col_shift + width].add(
            part
        )
    return result[:, 1:-1, 1:-1]


def temporal_forward(stacked, weight, frames):
    total = jnp.float32(0.0)
    for lag_step in range(3):
        window = stacked[lag_step : lag_step + frames].reshape(-1, stacked.shape[3])
        total = total + jnp.dot(window, weight[lag_step], preferred_element_type=jnp.float32)
    return total


def temporal_transpose(grad_flat, weight, frames, height, width):
    total = jnp.zeros((frames + 2, height, width, weight.shape[1]), jnp.float32)
    for lag_step in range(3):
        part = contract_cols(grad_flat, weight[lag_step]).reshape(
            frames, height, width, weight.shape[1]
        )
        total = total + jnp.pad(part, ((lag_step, 2 - lag_step), (0, 0), (0, 0), (0, 0)))
    return total


def weight_grads(padded_act, stacked, grad_frames, upstream_frames, frames, height, width):
    columns = grad_frames.shape[-1]
    channels = padded_act.shape[-1]
    upstream_flat = upstream_frames.reshape(-1, columns)
    grad_t = jnp.stack(
        [
            contract_rows(
                stacked[lag_step : lag_step + frames].reshape(-1, channels), upstream_flat
            )
            for lag_step in range(3)
        ]
    )
    collected = []
    for row_shift, col_shift in spatial_taps:
        window = padded_act[
            :, row_shift : row_shift + height, col_shift : col_shift + width
        ].reshape(-1, channels)
        collected.append(contract_rows(window, grad_frames))
    return (jnp.stack(collected), grad_t)


def per_device(frames_in, cotangent, w_spatial, w_temporal):
    source = frames_in[0]
    upstream = cotangent[0]
    frames = 2 * source.shape[0]
    height, width, channels = (source.shape[1], source.shape[2], source.shape[3])
    voxels = frames * height * width
    first_device = lax.axis_index("tm") == 0
    upsampled = jnp.repeat(source, 2, axis=0)
    up_float = upsampled.astype(jnp.float32)
    activated = jax.nn.silu(up_float).astype(jnp.bfloat16)
    padded_act = jnp.pad(activated, ((0, 0), (1, 1), (1, 1), (0, 0)))
    columns = padded_act
    spatial_sum = spatial_forward(columns, lax.all_gather(w_spatial, "dp", axis=1, tiled=True))
    spatial_out = spatial_sum.reshape(frames, height, width, channels).astype(jnp.bfloat16)
    previous = passed_along(spatial_out[frames - 2 :], "tm", 1)
    previous = jnp.where(first_device, jnp.broadcast_to(spatial_out[:1], previous.shape), previous)
    stacked = jnp.concatenate([previous, spatial_out], axis=0)
    columns = stacked
    temporal_sum = temporal_forward(
        columns, lax.all_gather(w_temporal, "dp", axis=1, tiled=True), frames
    )
    decoded = (up_float + temporal_sum.reshape(frames, height, width, channels)).astype(
        jnp.bfloat16
    )
    following = passed_along(upstream[:2], "tm", -1)
    extended_flat = jnp.concatenate([upstream, following], axis=0).reshape(-1, channels)
    piece = lax.all_gather(w_temporal, "dp", axis=1, tiled=True)
    pad_grad = temporal_transpose(extended_flat, piece, frames + 2, height, width)
    inner = pad_grad[2 : frames + 2]
    edge = jnp.where(first_device, pad_grad[0] + pad_grad[1], jnp.zeros_like(pad_grad[0]))
    inner = inner.at[0].add(edge)
    inner_grad = inner.reshape(voxels, piece.shape[1])
    spatial_grad = inner_grad.astype(jnp.bfloat16)
    grad_s_local, grad_t_local = weight_grads(
        padded_act, stacked, spatial_grad, upstream, frames, height, width
    )
    owned_s, owned_t = (
        lax.psum_scatter(grad_s_local, "dp", scatter_dimension=1, tiled=True),
        lax.psum_scatter(grad_t_local, "dp", scatter_dimension=1, tiled=True),
    )
    summed_s, summed_t = lax.psum((owned_s, owned_t), "tm")
    piece = lax.all_gather(w_spatial, "dp", axis=1, tiled=True)
    act_flat = spatial_transpose(spatial_grad, piece, frames, height, width).reshape(
        voxels, piece.shape[1]
    )
    act_grad = act_flat.reshape(frames, height, width, channels)
    up_grad = upstream.astype(jnp.float32) + act_grad * silu_slope(up_float)
    grad_input = (
        up_grad.reshape(frames // 2, 2, height, width, channels).sum(axis=1).astype(jnp.bfloat16)
    )
    inverse = 1.0 / math.sqrt(lax.axis_size("dp") * lax.axis_size("tm") * voxels)
    return (decoded[None], grad_input[None], summed_s * inverse, summed_t * inverse)


def places(line, rows):
    index = lax.axis_index("dp")
    core = lax.rem(index, 2)
    row = lax.rem(index // 2, rows)
    return index // (2 * rows), row, core, lax.axis_index("tm")


def block_of(line, row, core, rows):
    return (line * rows + row) * 2 + core


def greet(peers):
    barrier = pltpu.get_barrier_semaphore()
    for peer in peers:
        pl.semaphore_signal(barrier, inc=1, device_id=peer, device_id_type=MESH)
    pl.semaphore_wait(barrier, len(peers))


def peers_of(line, row, core, tm, rows):
    along = [
        (block_of(lax.rem(line + step, LINE), row, core, rows), tm) for step in range(1, LINE)
    ]
    across = [
        (block_of(line, lax.rem(row + step, rows), core, rows), tm) for step in range(1, rows)
    ]
    sibling = (block_of(line, row, 1 - core, rows), tm)
    partner = (block_of(line, row, core, rows), 1 - tm)
    return along, across, sibling, partner


def wide_dot(left, right):
    return jnp.dot(left, right, preferred_element_type=jnp.float32)


def column_shifts(flat, width):
    count = flat.shape[0]
    column = lax.rem(lax.broadcasted_iota(jnp.int32, flat.shape, 0), width)
    left = jnp.where(column == 0, 0.0, pltpu.roll(flat, 1, 0))
    right = jnp.where(column == width - 1, 0.0, pltpu.roll(flat, count - 1, 0))
    return left, flat, right


def fill_columns(target, place, flat, width, flip):
    channels = flat.shape[1]
    shifts = column_shifts(flat, width)
    for number, value in enumerate(shifts[::-1] if flip else shifts):
        target[place : place + flat.shape[0], number * channels : (number + 1) * channels] = (
            value.astype(jnp.bfloat16)
        )


def up_to(count, step):
    return -(-count // step) * step


def section_kernel(
    rows,
    width,
    wt_ref,
    ws_ref,
    u_ref,
    c_ref,
    decoded_ref,
    input_ref,
    gs_ref,
    gt_ref,
    out_ref,
    wt_all,
    ws_all,
    u_all,
    c_all,
    partial,
    columns,
    columns_t,
    s_ref,
    s_t,
    g_ref,
    even_ref,
    odd_ref,
    spread,
    total_ref,
    s_halves,
    act_total,
    act_out,
    act_in,
    from_core,
    to_row,
    from_row,
    to_line,
    from_line,
    send_sem,
    recv_sem,
    pair_send,
    pair_recv,
    own_sem,
    core_send,
    core_recv,
    row_send,
    row_recv,
    line_send,
    line_recv,
    last_send,
    last_recv,
):
    line, row, core, tm = places(LINE, rows)
    along, across, sibling, partner = peers_of(line, row, core, tm, rows)
    greet(along + across + [sibling, partner])
    taps = wt_ref.shape[0]
    me = block_of(line, row, core, rows)
    own, _, pixels, channels = c_ref.shape
    frames = 2 * own
    stride = pixels + width
    span = frames * stride - width
    half = partial.shape[3]
    lanes = pl.ds(pl.multiple_of(tm * half, half), half)
    wide = jnp.float32
    narrow = jnp.bfloat16
    sent = []

    def remote(source, target, send, recv, peer):
        copy = pltpu.make_async_remote_copy(
            src_ref=source,
            dst_ref=target,
            send_sem=send,
            recv_sem=recv,
            device_id=peer,
            device_id_type=MESH,
        )
        copy.start()
        return copy

    def place_of(part, block):
        if part == 0:
            return wt_all.at[:, block]
        return ws_all.at[pl.ds((part - 1) * taps, taps), block]

    def push(part, source, block, peer, slot):
        sent.append(
            remote(source, place_of(part, block), send_sem.at[part, slot], recv_sem.at[part, block], peer)
        )

    def landed(part, block):
        view = place_of(part, block)
        pltpu.make_async_copy(view, view, recv_sem.at[part, block]).wait()
        return view

    first_across = LINE - 1
    first_core = first_across + LINE * (rows - 1)

    def push_own(part):
        block = wt_ref if part == 0 else ws_ref.at[pl.ds((part - 1) * taps, taps), :, lanes]
        for step, peer in enumerate(along):
            push(part, block, me, peer, step)
        for step, peer in enumerate(across):
            push(part, block, me, peer, first_across + step)
        push(part, block, me, sibling, first_core)

    def relay_line(part):
        for step in range(1, LINE):
            block = block_of(lax.rem(line + step, LINE), row, core, rows)
            view = landed(part, block)
            for number, peer in enumerate(across):
                push(part, view, block, peer, first_across + step * (rows - 1) + number)
            push(part, view, block, sibling, first_core + step)

    def relay_rows(part):
        for number in range(1, rows):
            for step in range(LINE):
                block = block_of(
                    lax.rem(line + step, LINE), lax.rem(row + number, rows), core, rows
                )
                push(part, landed(part, block), block, sibling, first_core + number * LINE + step)

    def complete(part):
        for number in range(rows):
            for step in range(LINE):
                landed(part, block_of(step, number, 1 - core, rows))

    def tap(number):
        return wt_all[number].reshape(channels, channels)

    order = list(range(1, LINE)) + [0]
    core_copies, row_copies, line_copies, last_copies = {}, {}, {}, []
    groups = ((3, 9), (0, 3))

    def sum_core(group):
        chosen = pl.ds(*groups[group])
        for number in list(range(1, rows)) + [0]:
            for step in order:
                slot = number * LINE + step
                block = block_of(
                    lax.rem(line + step, LINE), lax.rem(row + number, rows), 1 - core, rows
                )
                core_copies[group, slot] = remote(
                    partial.at[block, chosen],
                    from_core.at[slot, chosen],
                    core_send.at[group, slot],
                    core_recv.at[group, slot],
                    sibling,
                )

    def of_chip(group, number, step):
        chosen = pl.ds(*groups[group])
        slot = number * LINE + step
        block = block_of(lax.rem(line + step, LINE), lax.rem(row + number, rows), core, rows)
        core_copies[group, slot].wait_recv()
        return partial[block, chosen].astype(wide) + from_core[slot, chosen].astype(wide)

    def sum_rows(group):
        chosen = pl.ds(*groups[group])
        for number in range(1, rows):
            for step in order:
                slot = number * LINE + step
                to_row[slot, chosen] = of_chip(group, number, step).astype(narrow)
                row_copies[group, slot] = remote(
                    to_row.at[slot, chosen],
                    from_row.at[slot, chosen],
                    row_send.at[group, slot],
                    row_recv.at[group, slot],
                    across[number - 1],
                )

    def of_rows(group, step):
        value = of_chip(group, 0, step)
        for number in range(1, rows):
            slot = number * LINE + step
            row_copies[group, slot].wait_recv()
            value = value + from_row[slot, pl.ds(*groups[group])].astype(wide)
        return value

    def sum_line(group):
        chosen = pl.ds(*groups[group])
        for step in range(1, LINE):
            to_line[step, chosen] = of_rows(group, step).astype(narrow)
            line_copies[group, step] = remote(
                to_line.at[step, chosen],
                from_line.at[step, chosen],
                line_send.at[group, step],
                line_recv.at[group, step],
                along[step - 1],
            )

    def sum_last(group):
        chosen = pl.ds(*groups[group])
        value = of_rows(group, 0)
        for step in range(1, LINE):
            line_copies[group, step].wait_recv()
            value = value + from_line[step, chosen].astype(wide)
        out_ref[tm, chosen] = value.astype(narrow)
        view = out_ref.at[tm, chosen]
        last_copies.append(
            remote(view, view, last_send.at[group], last_recv.at[group], partner)
        )

    def store(number, value):
        partial[:, number] = value.astype(narrow).reshape(
            partial.shape[0], partial.shape[2], half
        )

    def lay_out():
        for frame in range(frames):
            value = u_all[frame // own, frame % own].astype(wide)
            fill_columns(
                columns, width + frame * stride, value / (1.0 + jnp.exp(-value)), width, False
            )
            place = slice((frame + 1) * pixels, (frame + 2) * pixels)
            even_ref[place] = c_all[frame // own, frame % own, 0]
            odd_ref[place] = c_all[frame // own, frame % own, 1]
        columns_t[...] = columns[...].T

    def temporal_back():
        even = even_ref[pixels : (frames + 1) * pixels]
        odd = odd_ref[pixels : (frames + 1) * pixels]
        here = contract_cols(even, tap(2)) + contract_cols(odd, tap(2))
        here = here + contract_cols(odd, tap(1))
        ahead = contract_cols(even, tap(0)) + contract_cols(odd, tap(0))
        ahead = ahead + contract_cols(even, tap(1))
        for frame in range(frames):
            value = here[frame * pixels : (frame + 1) * pixels]
            if frame == 0:
                value = value + ahead[:pixels]
            if frame < frames - 1:
                value = value + ahead[(frame + 1) * pixels : (frame + 2) * pixels]
            place = 2 * width + frame * stride
            g_ref[place : place + pixels] = value.astype(narrow)

    def spatial_weight_grads():
        depth = columns.shape[0]
        for r in range(3):
            begin = (2 - r) * width
            value = wide_dot(columns_t[...], g_ref[begin : begin + depth, lanes])
            for s in range(3):
                store(3 + 3 * r + s, value[s * channels : (s + 1) * channels])

    def spatial_row(r):
        value = wide_dot(
            columns[r * width : r * width + span],
            ws_all[3 * r : 3 * r + 3].reshape(3 * channels, half),
        )
        total_ref[...] = value if r == 0 else total_ref[...] + value

    def spatial_done():
        for frame in range(frames):
            value = total_ref[frame * stride : frame * stride + pixels].astype(narrow)
            s_halves[tm, frame * pixels : (frame + 1) * pixels] = value
        view = s_halves.at[tm]
        pairs.append(remote(view, view, pair_send.at[2], pair_recv.at[2], partner))

    def spatial_join():
        pairs[2].wait_recv()
        for side in range(2):
            columns_of = slice(side * half, (side + 1) * half)
            s_ref[pixels : (frames + 1) * pixels, columns_of] = s_halves[side]
            s_ref[:pixels, columns_of] = s_halves[side, :pixels]

    def temporal_weight_grads():
        s_t[...] = s_ref[...].T
        extent = s_ref.shape[0]
        past_even = wide_dot(s_t[...], even_ref[pixels : pixels + extent, lanes])
        now_odd = wide_dot(s_t[...], odd_ref[:extent, lanes])
        store(1, past_even + now_odd)
        store(0, past_even + wide_dot(s_t[...], odd_ref[pixels : pixels + extent, lanes]))
        store(2, now_odd + wide_dot(s_t[...], even_ref[:extent, lanes]))

    def decode():
        start = tm * (own * pixels)
        past = s_ref[pl.ds(pl.multiple_of(start, 16), own * pixels)]
        now = s_ref[pl.ds(pl.multiple_of(start + pixels, 16), own * pixels)]
        base = wide_dot(past, tap(0)) + wide_dot(now, tap(2))
        first = base + wide_dot(past, tap(1))
        second = base + wide_dot(now, tap(1))
        for frame in range(own):
            place = slice(frame * pixels, (frame + 1) * pixels)
            value = u_all[tm, frame].astype(wide)
            decoded_ref[frame, 0] = (value + first[place]).astype(narrow)
            decoded_ref[frame, 1] = (value + second[place]).astype(narrow)

    def rows_of(side, frame):
        return pl.ds(pl.multiple_of((side * own + frame) * stride, 16), pixels)

    def spatial_back():
        for frame in range(frames):
            place = 2 * width + frame * stride
            flat = g_ref[place : place + pixels, lanes].astype(wide)
            fill_columns(spread, width + frame * stride, flat, width, True)
        value = jnp.zeros((span, channels), wide)
        for r in range(3):
            begin = (2 - r) * width
            for s in range(3):
                value = value + contract_cols(
                    spread[begin : begin + span, s * half : (s + 1) * half],
                    ws_all[3 * r + s].reshape(channels, half),
                )
        act_total[...] = value
        for frame in range(own):
            act_out[frame] = act_total[rows_of(1 - tm, frame)].astype(narrow)
        pairs.append(remote(act_out, act_in, pair_send.at[3], pair_recv.at[3], partner))

    def input_grads():
        pairs[3].wait_recv()
        for frame in range(own):
            part = act_total[rows_of(tm, frame)] + act_in[frame].astype(wide)
            held = u_all[tm, frame].astype(wide)
            sigmoid = 1.0 / (1.0 + jnp.exp(-held))
            slope = sigmoid * (1.0 + held * (1.0 - sigmoid))
            pair = c_all[tm, frame, 0].astype(wide) + c_all[tm, frame, 1].astype(wide)
            input_ref[frame] = (pair + part * slope).astype(narrow)

    push_own(0)
    pairs = [
        remote(u_ref, u_all.at[tm], pair_send.at[0], pair_recv.at[0], partner),
        remote(c_ref, c_all.at[tm], pair_send.at[1], pair_recv.at[1], partner),
    ]
    for part in range(1, PARTS):
        push_own(part)
    kept = [
        pltpu.make_async_copy(wt_ref, wt_all.at[:, me], own_sem.at[0]),
        pltpu.make_async_copy(ws_ref.at[:, :, lanes], ws_all.at[:, me], own_sem.at[3]),
        pltpu.make_async_copy(u_ref, u_all.at[tm], own_sem.at[1]),
        pltpu.make_async_copy(c_ref, c_all.at[tm], own_sem.at[2]),
    ]
    for copy in kept:
        copy.start()
    for scratch in (columns, s_ref, g_ref, even_ref, odd_ref, spread):
        scratch[...] = jnp.zeros_like(scratch)
    relay_line(0)
    relay_line(1)
    relay_rows(0)
    for copy in kept:
        copy.wait()
    for copy in pairs:
        copy.wait_recv()
    lay_out()
    relay_line(2)
    relay_rows(1)
    complete(0)
    temporal_back()
    relay_line(3)
    relay_rows(2)
    spatial_weight_grads()
    sum_core(0)
    complete(1)
    spatial_row(0)
    relay_rows(3)
    sum_rows(0)
    complete(2)
    spatial_row(1)
    complete(3)
    spatial_row(2)
    spatial_done()
    spatial_back()
    sum_line(0)
    spatial_join()
    temporal_weight_grads()
    sum_core(1)
    sum_rows(1)
    decode()
    sum_line(1)
    input_grads()
    sum_last(0)
    sum_last(1)
    for copy in sent + pairs:
        copy.wait_send()
    for copies in (core_copies, row_copies, line_copies):
        for copy in copies.values():
            copy.wait_send()
    for copy in last_copies:
        copy.wait()
    for side in range(2):
        gt_ref[:, :, side * half : (side + 1) * half] = out_ref[side, :taps]
        gs_ref[:, :, side * half : (side + 1) * half] = out_ref[side, taps:]


def section(w_temporal, w_spatial, source, upstream, width, devices):
    rows = devices // (2 * LINE)
    own, pixels, channels = source.shape
    block = w_temporal.shape[1]
    taps = w_temporal.shape[0] + w_spatial.shape[0]
    frames, half = 2 * own, channels // 2
    stride = pixels + width
    depth = up_to(width + frames * stride, 256)
    extent = up_to((frames + 1) * pixels, 128)
    many = rows * LINE
    slots = (LINE - 1) + LINE * (rows - 1) + many
    kept = source.dtype
    anywhere = pl.BlockSpec(memory_space=pl.ANY)
    in_vmem = pl.BlockSpec(memory_space=pltpu.VMEM)
    dma = pltpu.SemaphoreType.DMA
    return pl.pallas_call(
        functools.partial(section_kernel, rows, width),
        out_shape=(
            jax.ShapeDtypeStruct((own, 2, pixels, channels), kept),
            jax.ShapeDtypeStruct((own, pixels, channels), kept),
            jax.ShapeDtypeStruct(w_spatial.shape, kept),
            jax.ShapeDtypeStruct(w_temporal.shape, kept),
        ),
        in_specs=[anywhere] * 4,
        out_specs=(in_vmem,) * 4,
        scratch_shapes=[
            pltpu.VMEM((2, taps, block, half), kept),
            pltpu.VMEM((w_temporal.shape[0], devices, block, channels), kept),
            pltpu.VMEM((w_spatial.shape[0], devices, block, half), kept),
            pltpu.VMEM((2, own, pixels, channels), kept),
            pltpu.VMEM((2, own, 2, pixels, channels), kept),
            pltpu.VMEM((devices, taps, block, half), kept),
            pltpu.VMEM((depth, 3 * channels), kept),
            pltpu.VMEM((3 * channels, depth), kept),
            pltpu.VMEM((extent, channels), kept),
            pltpu.VMEM((channels, extent), kept),
            pltpu.VMEM((depth + 2 * width, channels), kept),
            pltpu.VMEM((extent + pixels, channels), kept),
            pltpu.VMEM((extent + pixels, channels), kept),
            pltpu.VMEM((width + frames * stride, 3 * half), kept),
            pltpu.VMEM((frames * stride - width, half), jnp.float32),
            pltpu.VMEM((2, frames * pixels, half), kept),
            pltpu.VMEM((frames * stride - width, channels), jnp.float32),
            pltpu.VMEM((own, pixels, channels), kept),
            pltpu.VMEM((own, pixels, channels), kept),
            pltpu.VMEM((many, taps, block, half), kept),
            pltpu.VMEM((many, taps, block, half), kept),
            pltpu.VMEM((many, taps, block, half), kept),
            pltpu.VMEM((LINE, taps, block, half), kept),
            pltpu.VMEM((LINE, taps, block, half), kept),
            dma((PARTS, slots)),
            dma((PARTS, devices)),
            dma((4,)),
            dma((4,)),
            dma((4,)),
            dma((2, many)),
            dma((2, many)),
            dma((2, many)),
            dma((2, many)),
            dma((2, LINE)),
            dma((2, LINE)),
            dma((2,)),
            dma((2,)),
        ],
        compiler_params=pltpu.CompilerParams(
            collective_id=0, has_side_effects=True, vmem_limit_bytes=58 * 2**20
        ),
        cost_estimate=pl.CostEstimate(
            flops=20 * frames * pixels * channels * channels * 2,
            bytes_accessed=12 * 2**20,
            transcendentals=2 * frames * pixels * channels,
        ),
        name="section",
    )(w_temporal, w_spatial, source, upstream)


def paired_device(frames_in, cotangent, w_spatial, w_temporal):
    devices = lax.axis_size("dp")
    source = frames_in[0]
    own, height, width, channels = source.shape
    frames, pixels = 2 * own, height * width
    decoded, grad_input, grad_s, grad_t = section(
        w_temporal,
        w_spatial,
        source.reshape(own, pixels, channels),
        cotangent[0].reshape(own, 2, pixels, channels),
        width,
        devices,
    )
    inverse = 1.0 / math.sqrt(devices * 2 * frames * pixels)
    return (
        decoded.reshape(1, 2 * own, height, width, channels),
        grad_input.reshape(1, own, height, width, channels),
        grad_s.astype(jnp.float32) * inverse,
        grad_t.astype(jnp.float32) * inverse,
    )


def solution(mesh):
    clip_split = P("dp", "tm", None, None, None)
    rows_split = P(None, "dp", None)
    paired = mesh.shape["tm"] == 2 and mesh.shape["dp"] % (2 * LINE) == 0
    return jax.shard_map(
        paired_device if paired else per_device,
        mesh=mesh,
        in_specs=(clip_split, clip_split, rows_split, rows_split),
        out_specs=(clip_split, clip_split, rows_split, rows_split),
        check_vma=False,
    )
```

```python
import functools
import math

import jax
import jax.numpy as jnp
from jax import lax
from jax.experimental import pallas as pl
from jax.experimental.pallas import tpu as pltpu
from jax.sharding import PartitionSpec as P

MESH = pl.DeviceIdType.MESH
LINE = 4
PARTS = 4

spatial_taps = [(row_shift, col_shift) for row_shift in range(3) for col_shift in range(3)]


def passed_along(value, axis, steps):
    count = lax.axis_size(axis)
    leading, last = (max(0, -steps), min(count, count - steps))
    return lax.ppermute(value, axis, [(source, source + steps) for source in range(leading, last)])


def contract_rows(left, right):
    return lax.dot_general(
        left, right, (((0,), (0,)), ((), ())), preferred_element_type=jnp.float32
    )


def contract_cols(left, right):
    return lax.dot_general(
        left, right, (((1,), (1,)), ((), ())), preferred_element_type=jnp.float32
    )


def silu_slope(value):
    sigmoid = jax.nn.sigmoid(value)
    return sigmoid * (1.0 + value * (1.0 - sigmoid))


def spatial_forward(padded_act, weight):
    height = padded_act.shape[1] - 2
    width = padded_act.shape[2] - 2
    total = jnp.float32(0.0)
    for position, (row_shift, col_shift) in enumerate(spatial_taps):
        window = padded_act[
            :, row_shift : row_shift + height, col_shift : col_shift + width
        ].reshape(-1, padded_act.shape[3])
        total = total + jnp.dot(window, weight[position], preferred_element_type=jnp.float32)
    return total


def spatial_transpose(grad_flat, weight, frames, height, width):
    result = jnp.zeros((frames, height + 2, width + 2, weight.shape[1]), jnp.float32)
    for position, (row_shift, col_shift) in enumerate(spatial_taps):
        part = contract_cols(grad_flat, weight[position]).reshape(
            frames, height, width, weight.shape[1]
        )
        result = result.at[:, row_shift : row_shift + height, col_shift : col_shift + width].add(
            part
        )
    return result[:, 1:-1, 1:-1]


def temporal_forward(stacked, weight, frames):
    total = jnp.float32(0.0)
    for lag_step in range(3):
        window = stacked[lag_step : lag_step + frames].reshape(-1, stacked.shape[3])
        total = total + jnp.dot(window, weight[lag_step], preferred_element_type=jnp.float32)
    return total


def temporal_transpose(grad_flat, weight, frames, height, width):
    total = jnp.zeros((frames + 2, height, width, weight.shape[1]), jnp.float32)
    for lag_step in range(3):
        part = contract_cols(grad_flat, weight[lag_step]).reshape(
            frames, height, width, weight.shape[1]
        )
        total = total + jnp.pad(part, ((lag_step, 2 - lag_step), (0, 0), (0, 0), (0, 0)))
    return total


def weight_grads(padded_act, stacked, grad_frames, upstream_frames, frames, height, width):
    columns = grad_frames.shape[-1]
    channels = padded_act.shape[-1]
    upstream_flat = upstream_frames.reshape(-1, columns)
    grad_t = jnp.stack(
        [
            contract_rows(
                stacked[lag_step : lag_step + frames].reshape(-1, channels), upstream_flat
            )
            for lag_step in range(3)
        ]
    )
    collected = []
    for row_shift, col_shift in spatial_taps:
        window = padded_act[
            :, row_shift : row_shift + height, col_shift : col_shift + width
        ].reshape(-1, channels)
        collected.append(contract_rows(window, grad_frames))
    return (jnp.stack(collected), grad_t)


def per_device(frames_in, cotangent, w_spatial, w_temporal):
    source = frames_in[0]
    upstream = cotangent[0]
    frames = 2 * source.shape[0]
    height, width, channels = (source.shape[1], source.shape[2], source.shape[3])
    voxels = frames * height * width
    first_device = lax.axis_index("tm") == 0
    upsampled = jnp.repeat(source, 2, axis=0)
    up_float = upsampled.astype(jnp.float32)
    activated = jax.nn.silu(up_float).astype(jnp.bfloat16)
    padded_act = jnp.pad(activated, ((0, 0), (1, 1), (1, 1), (0, 0)))
    columns = padded_act
    spatial_sum = spatial_forward(columns, lax.all_gather(w_spatial, "dp", axis=1, tiled=True))
    spatial_out = spatial_sum.reshape(frames, height, width, channels).astype(jnp.bfloat16)
    previous = passed_along(spatial_out[frames - 2 :], "tm", 1)
    previous = jnp.where(first_device, jnp.broadcast_to(spatial_out[:1], previous.shape), previous)
    stacked = jnp.concatenate([previous, spatial_out], axis=0)
    columns = stacked
    temporal_sum = temporal_forward(
        columns, lax.all_gather(w_temporal, "dp", axis=1, tiled=True), frames
    )
    decoded = (up_float + temporal_sum.reshape(frames, height, width, channels)).astype(
        jnp.bfloat16
    )
    following = passed_along(upstream[:2], "tm", -1)
    extended_flat = jnp.concatenate([upstream, following], axis=0).reshape(-1, channels)
    piece = lax.all_gather(w_temporal, "dp", axis=1, tiled=True)
    pad_grad = temporal_transpose(extended_flat, piece, frames + 2, height, width)
    inner = pad_grad[2 : frames + 2]
    edge = jnp.where(first_device, pad_grad[0] + pad_grad[1], jnp.zeros_like(pad_grad[0]))
    inner = inner.at[0].add(edge)
    inner_grad = inner.reshape(voxels, piece.shape[1])
    spatial_grad = inner_grad.astype(jnp.bfloat16)
    grad_s_local, grad_t_local = weight_grads(
        padded_act, stacked, spatial_grad, upstream, frames, height, width
    )
    owned_s, owned_t = (
        lax.psum_scatter(grad_s_local, "dp", scatter_dimension=1, tiled=True),
        lax.psum_scatter(grad_t_local, "dp", scatter_dimension=1, tiled=True),
    )
    summed_s, summed_t = lax.psum((owned_s, owned_t), "tm")
    piece = lax.all_gather(w_spatial, "dp", axis=1, tiled=True)
    act_flat = spatial_transpose(spatial_grad, piece, frames, height, width).reshape(
        voxels, piece.shape[1]
    )
    act_grad = act_flat.reshape(frames, height, width, channels)
    up_grad = upstream.astype(jnp.float32) + act_grad * silu_slope(up_float)
    grad_input = (
        up_grad.reshape(frames // 2, 2, height, width, channels).sum(axis=1).astype(jnp.bfloat16)
    )
    inverse = 1.0 / math.sqrt(lax.axis_size("dp") * lax.axis_size("tm") * voxels)
    return (decoded[None], grad_input[None], summed_s * inverse, summed_t * inverse)


def places(line, rows):
    index = lax.axis_index("dp")
    core = lax.rem(index, 2)
    row = lax.rem(index // 2, rows)
    return index // (2 * rows), row, core, lax.axis_index("tm")


def block_of(line, row, core, rows):
    return (line * rows + row) * 2 + core


def greet(peers):
    barrier = pltpu.get_barrier_semaphore()
    for peer in peers:
        pl.semaphore_signal(barrier, inc=1, device_id=peer, device_id_type=MESH)
    pl.semaphore_wait(barrier, len(peers))


def peers_of(line, row, core, tm, rows):
    along = [
        (block_of(lax.rem(line + step, LINE), row, core, rows), tm) for step in range(1, LINE)
    ]
    across = [
        (block_of(line, lax.rem(row + step, rows), core, rows), tm) for step in range(1, rows)
    ]
    sibling = (block_of(line, row, 1 - core, rows), tm)
    partner = (block_of(line, row, core, rows), 1 - tm)
    return along, across, sibling, partner


def wide_dot(left, right):
    return jnp.dot(left, right, preferred_element_type=jnp.float32)


def column_shifts(flat, width):
    count = flat.shape[0]
    column = lax.rem(lax.broadcasted_iota(jnp.int32, flat.shape, 0), width)
    left = jnp.where(column == 0, 0.0, pltpu.roll(flat, 1, 0))
    right = jnp.where(column == width - 1, 0.0, pltpu.roll(flat, count - 1, 0))
    return left, flat, right


def fill_columns(target, place, flat, width, flip):
    channels = flat.shape[1]
    shifts = column_shifts(flat, width)
    for number, value in enumerate(shifts[::-1] if flip else shifts):
        target[place : place + flat.shape[0], number * channels : (number + 1) * channels] = (
            value.astype(jnp.bfloat16)
        )


def up_to(count, step):
    return -(-count // step) * step


def section_kernel(
    rows,
    width,
    inverse,
    wt_ref,
    ws_ref,
    u_ref,
    c_ref,
    decoded_ref,
    input_ref,
    gs_ref,
    gt_ref,
    out_ref,
    wt_all,
    ws_all,
    u_all,
    c_all,
    partial,
    columns,
    columns_t,
    s_ref,
    s_t,
    g_ref,
    even_ref,
    odd_ref,
    spread,
    total_ref,
    s_halves,
    act_total,
    act_out,
    act_in,
    from_core,
    to_row,
    from_row,
    to_line,
    from_line,
    send_sem,
    recv_sem,
    pair_send,
    pair_recv,
    own_sem,
    core_send,
    core_recv,
    row_send,
    row_recv,
    line_send,
    line_recv,
    last_send,
    last_recv,
):
    line, row, core, tm = places(LINE, rows)
    along, across, sibling, partner = peers_of(line, row, core, tm, rows)
    greet(along + across + [sibling, partner])
    taps = wt_ref.shape[0]
    me = block_of(line, row, core, rows)
    own, _, pixels, channels = c_ref.shape
    frames = 2 * own
    stride = pixels + width
    span = frames * stride - width
    half = partial.shape[3]
    lanes = pl.ds(pl.multiple_of(tm * half, half), half)
    wide = jnp.float32
    narrow = jnp.bfloat16
    sent = []

    def remote(source, target, send, recv, peer):
        copy = pltpu.make_async_remote_copy(
            src_ref=source,
            dst_ref=target,
            send_sem=send,
            recv_sem=recv,
            device_id=peer,
            device_id_type=MESH,
        )
        copy.start()
        return copy

    def place_of(part, block):
        if part == 0:
            return wt_all.at[:, block]
        return ws_all.at[pl.ds((part - 1) * taps, taps), block]

    def push(part, source, block, peer, slot):
        sent.append(
            remote(source, place_of(part, block), send_sem.at[part, slot], recv_sem.at[part, block], peer)
        )

    def landed(part, block):
        view = place_of(part, block)
        pltpu.make_async_copy(view, view, recv_sem.at[part, block]).wait()
        return view

    first_across = LINE - 1
    first_core = first_across + LINE * (rows - 1)

    def push_own(part):
        block = wt_ref if part == 0 else ws_ref.at[pl.ds((part - 1) * taps, taps), :, lanes]
        for step, peer in enumerate(along):
            push(part, block, me, peer, step)
        for step, peer in enumerate(across):
            push(part, block, me, peer, first_across + step)
        push(part, block, me, sibling, first_core)

    def relay_line(part):
        for step in range(1, LINE):
            block = block_of(lax.rem(line + step, LINE), row, core, rows)
            view = landed(part, block)
            for number, peer in enumerate(across):
                push(part, view, block, peer, first_across + step * (rows - 1) + number)
            push(part, view, block, sibling, first_core + step)

    def relay_rows(part):
        for number in range(1, rows):
            for step in range(LINE):
                block = block_of(
                    lax.rem(line + step, LINE), lax.rem(row + number, rows), core, rows
                )
                push(part, landed(part, block), block, sibling, first_core + number * LINE + step)

    def complete(part):
        for number in range(rows):
            for step in range(LINE):
                landed(part, block_of(step, number, 1 - core, rows))

    def tap(number):
        return wt_all[number].reshape(channels, channels)

    order = list(range(1, LINE)) + [0]
    core_copies, row_copies, line_copies, last_copies = {}, {}, {}, []
    groups = ((3, 9), (0, 3))

    def sum_core(group):
        chosen = pl.ds(*groups[group])
        for number in list(range(1, rows)) + [0]:
            for step in order:
                slot = number * LINE + step
                block = block_of(
                    lax.rem(line + step, LINE), lax.rem(row + number, rows), 1 - core, rows
                )
                core_copies[group, slot] = remote(
                    partial.at[block, chosen],
                    from_core.at[slot, chosen],
                    core_send.at[group, slot],
                    core_recv.at[group, slot],
                    sibling,
                )

    def of_chip(group, number, step):
        chosen = pl.ds(*groups[group])
        slot = number * LINE + step
        block = block_of(lax.rem(line + step, LINE), lax.rem(row + number, rows), core, rows)
        core_copies[group, slot].wait_recv()
        return partial[block, chosen].astype(wide) + from_core[slot, chosen].astype(wide)

    def sum_rows(group):
        chosen = pl.ds(*groups[group])
        for number in range(1, rows):
            for step in order:
                slot = number * LINE + step
                to_row[slot, chosen] = of_chip(group, number, step).astype(narrow)
                row_copies[group, slot] = remote(
                    to_row.at[slot, chosen],
                    from_row.at[slot, chosen],
                    row_send.at[group, slot],
                    row_recv.at[group, slot],
                    across[number - 1],
                )

    def of_rows(group, step):
        value = of_chip(group, 0, step)
        for number in range(1, rows):
            slot = number * LINE + step
            row_copies[group, slot].wait_recv()
            value = value + from_row[slot, pl.ds(*groups[group])].astype(wide)
        return value

    def sum_line(group, steps):
        chosen = pl.ds(*groups[group])
        for step in steps:
            to_line[step, chosen] = of_rows(group, step).astype(narrow)
            line_copies[group, step] = remote(
                to_line.at[step, chosen],
                from_line.at[step, chosen],
                line_send.at[group, step],
                line_recv.at[group, step],
                along[step - 1],
            )

    def sum_last(group):
        chosen = pl.ds(*groups[group])
        value = of_rows(group, 0)
        for step in range(1, LINE):
            line_copies[group, step].wait_recv()
            value = value + from_line[step, chosen].astype(wide)
        out_ref[tm, chosen] = value.astype(narrow)
        view = out_ref.at[tm, chosen]
        last_copies.append(
            remote(view, view, last_send.at[group], last_recv.at[group], partner)
        )

    def store(number, value):
        partial[:, number] = value.astype(narrow).reshape(
            partial.shape[0], partial.shape[2], half
        )

    def lay_out():
        for frame in range(frames):
            value = u_all[frame // own, frame % own].astype(wide)
            fill_columns(
                columns, width + frame * stride, value / (1.0 + jnp.exp(-value)), width, False
            )
        columns_t[...] = columns[...].T

    def lay_out_grads():
        for frame in range(frames):
            place = slice((frame + 1) * pixels, (frame + 2) * pixels)
            even_ref[place] = c_all[frame // own, frame % own, 0]
            odd_ref[place] = c_all[frame // own, frame % own, 1]

    def temporal_back():
        even = even_ref[pixels : (frames + 1) * pixels]
        odd = odd_ref[pixels : (frames + 1) * pixels]
        here = contract_cols(even, tap(2)) + contract_cols(odd, tap(2))
        here = here + contract_cols(odd, tap(1))
        ahead = contract_cols(even, tap(0)) + contract_cols(odd, tap(0))
        ahead = ahead + contract_cols(even, tap(1))
        for frame in range(frames):
            value = here[frame * pixels : (frame + 1) * pixels]
            if frame == 0:
                value = value + ahead[:pixels]
            if frame < frames - 1:
                value = value + ahead[(frame + 1) * pixels : (frame + 2) * pixels]
            place = 2 * width + frame * stride
            g_ref[place : place + pixels] = value.astype(narrow)

    def spatial_weight_grads():
        depth = columns.shape[0]
        for r in range(3):
            begin = (2 - r) * width
            value = wide_dot(columns_t[...], g_ref[begin : begin + depth, lanes])
            for s in range(3):
                store(3 + 3 * r + s, value[s * channels : (s + 1) * channels])

    def spatial_row(r):
        value = wide_dot(
            columns[r * width : r * width + span],
            ws_all[3 * r : 3 * r + 3].reshape(3 * channels, half),
        )
        total_ref[...] = value if r == 0 else total_ref[...] + value

    def spatial_done():
        for frame in range(frames):
            value = total_ref[frame * stride : frame * stride + pixels].astype(narrow)
            s_halves[tm, frame * pixels : (frame + 1) * pixels] = value
        view = s_halves.at[tm]
        pairs.append(remote(view, view, pair_send.at[2], pair_recv.at[2], partner))

    def spatial_join():
        pairs[2].wait_recv()
        for side in range(2):
            columns_of = slice(side * half, (side + 1) * half)
            s_ref[pixels : (frames + 1) * pixels, columns_of] = s_halves[side]
            s_ref[:pixels, columns_of] = s_halves[side, :pixels]

    def temporal_weight_grads():
        s_t[...] = s_ref[...].T
        extent = s_ref.shape[0]
        past_even = wide_dot(s_t[...], even_ref[pixels : pixels + extent, lanes])
        now_odd = wide_dot(s_t[...], odd_ref[:extent, lanes])
        store(1, past_even + now_odd)
        store(0, past_even + wide_dot(s_t[...], odd_ref[pixels : pixels + extent, lanes]))
        store(2, now_odd + wide_dot(s_t[...], even_ref[:extent, lanes]))

    def decode():
        start = tm * (own * pixels)
        past = s_ref[pl.ds(pl.multiple_of(start, 16), own * pixels)]
        now = s_ref[pl.ds(pl.multiple_of(start + pixels, 16), own * pixels)]
        base = wide_dot(past, tap(0)) + wide_dot(now, tap(2))
        first = base + wide_dot(past, tap(1))
        second = base + wide_dot(now, tap(1))
        for frame in range(own):
            place = slice(frame * pixels, (frame + 1) * pixels)
            value = u_all[tm, frame].astype(wide)
            decoded_ref[frame, 0] = (value + first[place]).astype(narrow)
            decoded_ref[frame, 1] = (value + second[place]).astype(narrow)

    def rows_of(side, frame):
        return pl.ds(pl.multiple_of((side * own + frame) * stride, 16), pixels)

    def spatial_back():
        for frame in range(frames):
            place = 2 * width + frame * stride
            flat = g_ref[place : place + pixels, lanes].astype(wide)
            fill_columns(spread, width + frame * stride, flat, width, True)
        value = jnp.zeros((span, channels), wide)
        for r in range(3):
            begin = (2 - r) * width
            for s in range(3):
                value = value + contract_cols(
                    spread[begin : begin + span, s * half : (s + 1) * half],
                    ws_all[3 * r + s].reshape(channels, half),
                )
        act_total[...] = value
        for frame in range(own):
            act_out[frame] = act_total[rows_of(1 - tm, frame)].astype(narrow)
        pairs.append(remote(act_out, act_in, pair_send.at[3], pair_recv.at[3], partner))

    def input_grads():
        pairs[3].wait_recv()
        for frame in range(own):
            part = act_total[rows_of(tm, frame)] + act_in[frame].astype(wide)
            held = u_all[tm, frame].astype(wide)
            sigmoid = 1.0 / (1.0 + jnp.exp(-held))
            slope = sigmoid * (1.0 + held * (1.0 - sigmoid))
            pair = c_all[tm, frame, 0].astype(wide) + c_all[tm, frame, 1].astype(wide)
            input_ref[frame] = (pair + part * slope).astype(narrow)

    push_own(0)
    pairs = [
        remote(u_ref, u_all.at[tm], pair_send.at[0], pair_recv.at[0], partner),
        remote(c_ref, c_all.at[tm], pair_send.at[1], pair_recv.at[1], partner),
    ]
    for part in range(1, PARTS):
        push_own(part)
    kept = [
        pltpu.make_async_copy(wt_ref, wt_all.at[:, me], own_sem.at[0]),
        pltpu.make_async_copy(ws_ref.at[:, :, lanes], ws_all.at[:, me], own_sem.at[3]),
        pltpu.make_async_copy(u_ref, u_all.at[tm], own_sem.at[1]),
        pltpu.make_async_copy(c_ref, c_all.at[tm], own_sem.at[2]),
    ]
    for copy in kept:
        copy.start()
    for scratch in (columns, s_ref, g_ref, even_ref, odd_ref, spread):
        scratch[...] = jnp.zeros_like(scratch)
    relay_line(0)
    relay_line(1)
    relay_rows(0)
    relay_line(2)
    relay_rows(1)
    for copy in kept:
        copy.wait()
    pairs[0].wait_recv()
    lay_out()
    relay_line(3)
    relay_rows(2)
    pairs[1].wait_recv()
    lay_out_grads()
    complete(0)
    temporal_back()
    relay_rows(3)
    spatial_weight_grads()
    sum_core(0)
    complete(1)
    spatial_row(0)
    sum_rows(0)
    complete(2)
    spatial_row(1)
    complete(3)
    spatial_row(2)
    spatial_done()
    spatial_back()
    sum_line(0, range(1, LINE - 1))
    spatial_join()
    temporal_weight_grads()
    sum_core(1)
    sum_line(0, range(LINE - 1, LINE))
    sum_rows(1)
    decode()
    sum_line(1, range(1, LINE))
    input_grads()
    sum_last(0)
    sum_last(1)
    for copy in sent + pairs:
        copy.wait_send()
    for copies in (core_copies, row_copies, line_copies):
        for copy in copies.values():
            copy.wait_send()
    for copy in last_copies:
        copy.wait()
    for side in range(2):
        place = slice(side * half, (side + 1) * half)
        gt_ref[:, :, place] = out_ref[side, :taps].astype(wide) * inverse
        gs_ref[:, :, place] = out_ref[side, taps:].astype(wide) * inverse


def section(w_temporal, w_spatial, source, upstream, width, devices):
    rows = devices // (2 * LINE)
    own, pixels, channels = source.shape
    block = w_temporal.shape[1]
    taps = w_temporal.shape[0] + w_spatial.shape[0]
    frames, half = 2 * own, channels // 2
    stride = pixels + width
    depth = up_to(width + frames * stride, 256)
    extent = up_to((frames + 1) * pixels, 128)
    inverse = 1.0 / math.sqrt(devices * 2 * frames * pixels)
    many = rows * LINE
    slots = (LINE - 1) + LINE * (rows - 1) + many
    kept = source.dtype
    anywhere = pl.BlockSpec(memory_space=pl.ANY)
    in_vmem = pl.BlockSpec(memory_space=pltpu.VMEM)
    dma = pltpu.SemaphoreType.DMA
    return pl.pallas_call(
        functools.partial(section_kernel, rows, width, inverse),
        out_shape=(
            jax.ShapeDtypeStruct((own, 2, pixels, channels), kept),
            jax.ShapeDtypeStruct((own, pixels, channels), kept),
            jax.ShapeDtypeStruct(w_spatial.shape, jnp.float32),
            jax.ShapeDtypeStruct(w_temporal.shape, jnp.float32),
        ),
        in_specs=[anywhere] * 4,
        out_specs=(in_vmem,) * 4,
        scratch_shapes=[
            pltpu.VMEM((2, taps, block, half), kept),
            pltpu.VMEM((w_temporal.shape[0], devices, block, channels), kept),
            pltpu.VMEM((w_spatial.shape[0], devices, block, half), kept),
            pltpu.VMEM((2, own, pixels, channels), kept),
            pltpu.VMEM((2, own, 2, pixels, channels), kept),
            pltpu.VMEM((devices, taps, block, half), kept),
            pltpu.VMEM((depth, 3 * channels), kept),
            pltpu.VMEM((3 * channels, depth), kept),
            pltpu.VMEM((extent, channels), kept),
            pltpu.VMEM((channels, extent), kept),
            pltpu.VMEM((depth + 2 * width, channels), kept),
            pltpu.VMEM((extent + pixels, channels), kept),
            pltpu.VMEM((extent + pixels, channels), kept),
            pltpu.VMEM((width + frames * stride, 3 * half), kept),
            pltpu.VMEM((frames * stride - width, half), jnp.float32),
            pltpu.VMEM((2, frames * pixels, half), kept),
            pltpu.VMEM((frames * stride - width, channels), jnp.float32),
            pltpu.VMEM((own, pixels, channels), kept),
            pltpu.VMEM((own, pixels, channels), kept),
            pltpu.VMEM((many, taps, block, half), kept),
            pltpu.VMEM((many, taps, block, half), kept),
            pltpu.VMEM((many, taps, block, half), kept),
            pltpu.VMEM((LINE, taps, block, half), kept),
            pltpu.VMEM((LINE, taps, block, half), kept),
            dma((PARTS, slots)),
            dma((PARTS, devices)),
            dma((4,)),
            dma((4,)),
            dma((4,)),
            dma((2, many)),
            dma((2, many)),
            dma((2, many)),
            dma((2, many)),
            dma((2, LINE)),
            dma((2, LINE)),
            dma((2,)),
            dma((2,)),
        ],
        compiler_params=pltpu.CompilerParams(
            collective_id=0, has_side_effects=True, vmem_limit_bytes=58 * 2**20
        ),
        cost_estimate=pl.CostEstimate(
            flops=20 * frames * pixels * channels * channels * 2,
            bytes_accessed=12 * 2**20,
            transcendentals=2 * frames * pixels * channels,
        ),
        name="section",
    )(w_temporal, w_spatial, source, upstream)


def paired_device(frames_in, cotangent, w_spatial, w_temporal):
    devices = lax.axis_size("dp")
    source = frames_in[0]
    own, height, width, channels = source.shape
    pixels = height * width
    decoded, grad_input, grad_s, grad_t = section(
        w_temporal,
        w_spatial,
        source.reshape(own, pixels, channels),
        cotangent[0].reshape(own, 2, pixels, channels),
        width,
        devices,
    )
    return (
        decoded.reshape(1, 2 * own, height, width, channels),
        grad_input.reshape(1, own, height, width, channels),
        grad_s,
        grad_t,
    )


def solution(mesh):
    clip_split = P("dp", "tm", None, None, None)
    rows_split = P(None, "dp", None)
    paired = mesh.shape["tm"] == 2 and mesh.shape["dp"] % (2 * LINE) == 0
    return jax.shard_map(
        paired_device if paired else per_device,
        mesh=mesh,
        in_specs=(clip_split, clip_split, rows_split, rows_split),
        out_specs=(clip_split, clip_split, rows_split, rows_split),
        check_vma=False,
    )
```

```python
import functools
import math

import jax
import jax.numpy as jnp
from jax import lax
from jax.experimental import pallas as pl
from jax.experimental.pallas import tpu as pltpu
from jax.sharding import PartitionSpec as P

MESH = pl.DeviceIdType.MESH
LINE = 4
PARTS = 4

spatial_taps = [(row_shift, col_shift) for row_shift in range(3) for col_shift in range(3)]


def passed_along(value, axis, steps):
    count = lax.axis_size(axis)
    leading, last = (max(0, -steps), min(count, count - steps))
    return lax.ppermute(value, axis, [(source, source + steps) for source in range(leading, last)])


def contract_rows(left, right):
    return lax.dot_general(
        left, right, (((0,), (0,)), ((), ())), preferred_element_type=jnp.float32
    )


def contract_cols(left, right):
    return lax.dot_general(
        left, right, (((1,), (1,)), ((), ())), preferred_element_type=jnp.float32
    )


def silu_slope(value):
    sigmoid = jax.nn.sigmoid(value)
    return sigmoid * (1.0 + value * (1.0 - sigmoid))


def spatial_forward(padded_act, weight):
    height = padded_act.shape[1] - 2
    width = padded_act.shape[2] - 2
    total = jnp.float32(0.0)
    for position, (row_shift, col_shift) in enumerate(spatial_taps):
        window = padded_act[
            :, row_shift : row_shift + height, col_shift : col_shift + width
        ].reshape(-1, padded_act.shape[3])
        total = total + jnp.dot(window, weight[position], preferred_element_type=jnp.float32)
    return total


def spatial_transpose(grad_flat, weight, frames, height, width):
    result = jnp.zeros((frames, height + 2, width + 2, weight.shape[1]), jnp.float32)
    for position, (row_shift, col_shift) in enumerate(spatial_taps):
        part = contract_cols(grad_flat, weight[position]).reshape(
            frames, height, width, weight.shape[1]
        )
        result = result.at[:, row_shift : row_shift + height, col_shift : col_shift + width].add(
            part
        )
    return result[:, 1:-1, 1:-1]


def temporal_forward(stacked, weight, frames):
    total = jnp.float32(0.0)
    for lag_step in range(3):
        window = stacked[lag_step : lag_step + frames].reshape(-1, stacked.shape[3])
        total = total + jnp.dot(window, weight[lag_step], preferred_element_type=jnp.float32)
    return total


def temporal_transpose(grad_flat, weight, frames, height, width):
    total = jnp.zeros((frames + 2, height, width, weight.shape[1]), jnp.float32)
    for lag_step in range(3):
        part = contract_cols(grad_flat, weight[lag_step]).reshape(
            frames, height, width, weight.shape[1]
        )
        total = total + jnp.pad(part, ((lag_step, 2 - lag_step), (0, 0), (0, 0), (0, 0)))
    return total


def weight_grads(padded_act, stacked, grad_frames, upstream_frames, frames, height, width):
    columns = grad_frames.shape[-1]
    channels = padded_act.shape[-1]
    upstream_flat = upstream_frames.reshape(-1, columns)
    grad_t = jnp.stack(
        [
            contract_rows(
                stacked[lag_step : lag_step + frames].reshape(-1, channels), upstream_flat
            )
            for lag_step in range(3)
        ]
    )
    collected = []
    for row_shift, col_shift in spatial_taps:
        window = padded_act[
            :, row_shift : row_shift + height, col_shift : col_shift + width
        ].reshape(-1, channels)
        collected.append(contract_rows(window, grad_frames))
    return (jnp.stack(collected), grad_t)


def per_device(frames_in, cotangent, w_spatial, w_temporal):
    source = frames_in[0]
    upstream = cotangent[0]
    frames = 2 * source.shape[0]
    height, width, channels = (source.shape[1], source.shape[2], source.shape[3])
    voxels = frames * height * width
    first_device = lax.axis_index("tm") == 0
    upsampled = jnp.repeat(source, 2, axis=0)
    up_float = upsampled.astype(jnp.float32)
    activated = jax.nn.silu(up_float).astype(jnp.bfloat16)
    padded_act = jnp.pad(activated, ((0, 0), (1, 1), (1, 1), (0, 0)))
    columns = padded_act
    spatial_sum = spatial_forward(columns, lax.all_gather(w_spatial, "dp", axis=1, tiled=True))
    spatial_out = spatial_sum.reshape(frames, height, width, channels).astype(jnp.bfloat16)
    previous = passed_along(spatial_out[frames - 2 :], "tm", 1)
    previous = jnp.where(first_device, jnp.broadcast_to(spatial_out[:1], previous.shape), previous)
    stacked = jnp.concatenate([previous, spatial_out], axis=0)
    columns = stacked
    temporal_sum = temporal_forward(
        columns, lax.all_gather(w_temporal, "dp", axis=1, tiled=True), frames
    )
    decoded = (up_float + temporal_sum.reshape(frames, height, width, channels)).astype(
        jnp.bfloat16
    )
    following = passed_along(upstream[:2], "tm", -1)
    extended_flat = jnp.concatenate([upstream, following], axis=0).reshape(-1, channels)
    piece = lax.all_gather(w_temporal, "dp", axis=1, tiled=True)
    pad_grad = temporal_transpose(extended_flat, piece, frames + 2, height, width)
    inner = pad_grad[2 : frames + 2]
    edge = jnp.where(first_device, pad_grad[0] + pad_grad[1], jnp.zeros_like(pad_grad[0]))
    inner = inner.at[0].add(edge)
    inner_grad = inner.reshape(voxels, piece.shape[1])
    spatial_grad = inner_grad.astype(jnp.bfloat16)
    grad_s_local, grad_t_local = weight_grads(
        padded_act, stacked, spatial_grad, upstream, frames, height, width
    )
    owned_s, owned_t = (
        lax.psum_scatter(grad_s_local, "dp", scatter_dimension=1, tiled=True),
        lax.psum_scatter(grad_t_local, "dp", scatter_dimension=1, tiled=True),
    )
    summed_s, summed_t = lax.psum((owned_s, owned_t), "tm")
    piece = lax.all_gather(w_spatial, "dp", axis=1, tiled=True)
    act_flat = spatial_transpose(spatial_grad, piece, frames, height, width).reshape(
        voxels, piece.shape[1]
    )
    act_grad = act_flat.reshape(frames, height, width, channels)
    up_grad = upstream.astype(jnp.float32) + act_grad * silu_slope(up_float)
    grad_input = (
        up_grad.reshape(frames // 2, 2, height, width, channels).sum(axis=1).astype(jnp.bfloat16)
    )
    inverse = 1.0 / math.sqrt(lax.axis_size("dp") * lax.axis_size("tm") * voxels)
    return (decoded[None], grad_input[None], summed_s * inverse, summed_t * inverse)


def places(line, rows):
    index = lax.axis_index("dp")
    core = lax.rem(index, 2)
    row = lax.rem(index // 2, rows)
    return index // (2 * rows), row, core, lax.axis_index("tm")


def block_of(line, row, core, rows):
    return (line * rows + row) * 2 + core


def greet(peers):
    barrier = pltpu.get_barrier_semaphore()
    for peer in peers:
        pl.semaphore_signal(barrier, inc=1, device_id=peer, device_id_type=MESH)
    pl.semaphore_wait(barrier, len(peers))


def peers_of(line, row, core, tm, rows):
    along = [
        (block_of(lax.rem(line + step, LINE), row, core, rows), tm) for step in range(1, LINE)
    ]
    across = [
        (block_of(line, lax.rem(row + step, rows), core, rows), tm) for step in range(1, rows)
    ]
    sibling = (block_of(line, row, 1 - core, rows), tm)
    partner = (block_of(line, row, core, rows), 1 - tm)
    return along, across, sibling, partner


def wide_dot(left, right):
    return jnp.dot(left, right, preferred_element_type=jnp.float32)


def column_shifts(flat, width):
    count = flat.shape[0]
    column = lax.rem(lax.broadcasted_iota(jnp.int32, flat.shape, 0), width)
    left = jnp.where(column == 0, 0.0, pltpu.roll(flat, 1, 0))
    right = jnp.where(column == width - 1, 0.0, pltpu.roll(flat, count - 1, 0))
    return left, flat, right


def fill_columns(target, place, flat, width, flip):
    channels = flat.shape[1]
    shifts = column_shifts(flat, width)
    for number, value in enumerate(shifts[::-1] if flip else shifts):
        target[place : place + flat.shape[0], number * channels : (number + 1) * channels] = (
            value.astype(jnp.bfloat16)
        )


def up_to(count, step):
    return -(-count // step) * step


def section_kernel(
    rows,
    width,
    wt_ref,
    ws_ref,
    u_ref,
    c_ref,
    decoded_ref,
    input_ref,
    gs_ref,
    gt_ref,
    out_ref,
    wt_all,
    ws_all,
    u_all,
    c_all,
    partial,
    columns,
    columns_t,
    s_ref,
    s_t,
    g_ref,
    even_ref,
    odd_ref,
    spread,
    total_ref,
    s_halves,
    act_total,
    act_out,
    act_in,
    from_core,
    to_row,
    from_row,
    to_line,
    from_line,
    send_sem,
    recv_sem,
    pair_send,
    pair_recv,
    own_sem,
    core_send,
    core_recv,
    row_send,
    row_recv,
    line_send,
    line_recv,
    last_send,
    last_recv,
):
    line, row, core, tm = places(LINE, rows)
    along, across, sibling, partner = peers_of(line, row, core, tm, rows)
    greet(along + across + [sibling, partner])
    taps = wt_ref.shape[0]
    me = block_of(line, row, core, rows)
    own, _, pixels, channels = c_ref.shape
    frames = 2 * own
    stride = pixels + width
    span = frames * stride - width
    half = partial.shape[3]
    lanes = pl.ds(pl.multiple_of(tm * half, half), half)
    wide = jnp.float32
    narrow = jnp.bfloat16
    sent = []

    def remote(source, target, send, recv, peer):
        copy = pltpu.make_async_remote_copy(
            src_ref=source,
            dst_ref=target,
            send_sem=send,
            recv_sem=recv,
            device_id=peer,
            device_id_type=MESH,
        )
        copy.start()
        return copy

    def place_of(part, block):
        if part == 0:
            return wt_all.at[:, block]
        return ws_all.at[pl.ds((part - 1) * taps, taps), block]

    def push(part, source, block, peer, slot):
        sent.append(
            remote(source, place_of(part, block), send_sem.at[part, slot], recv_sem.at[part, block], peer)
        )

    def landed(part, block):
        view = place_of(part, block)
        pltpu.make_async_copy(view, view, recv_sem.at[part, block]).wait()
        return view

    first_across = LINE - 1
    first_core = first_across + LINE * (rows - 1)

    def push_own(part):
        block = wt_ref if part == 0 else ws_ref.at[pl.ds((part - 1) * taps, taps), :, lanes]
        for step, peer in enumerate(along):
            push(part, block, me, peer, step)
        for step, peer in enumerate(across):
            push(part, block, me, peer, first_across + step)
        push(part, block, me, sibling, first_core)

    def relay_line(part):
        for step in range(1, LINE):
            block = block_of(lax.rem(line + step, LINE), row, core, rows)
            view = landed(part, block)
            for number, peer in enumerate(across):
                push(part, view, block, peer, first_across + step * (rows - 1) + number)
            push(part, view, block, sibling, first_core + step)

    def relay_rows(part):
        for number in range(1, rows):
            for step in range(LINE):
                block = block_of(
                    lax.rem(line + step, LINE), lax.rem(row + number, rows), core, rows
                )
                push(part, landed(part, block), block, sibling, first_core + number * LINE + step)

    def complete(part):
        for number in range(rows):
            for step in range(LINE):
                landed(part, block_of(step, number, 1 - core, rows))

    def tap(number):
        return wt_all[number].reshape(channels, channels)

    order = list(range(1, LINE)) + [0]
    core_copies, row_copies, line_copies, last_copies = {}, {}, {}, []
    groups = ((3, 9), (0, 3))

    def sum_core(group):
        chosen = pl.ds(*groups[group])
        for number in list(range(1, rows)) + [0]:
            for step in order:
                slot = number * LINE + step
                block = block_of(
                    lax.rem(line + step, LINE), lax.rem(row + number, rows), 1 - core, rows
                )
                core_copies[group, slot] = remote(
                    partial.at[block, chosen],
                    from_core.at[slot, chosen],
                    core_send.at[group, slot],
                    core_recv.at[group, slot],
                    sibling,
                )

    def of_chip(group, number, step):
        chosen = pl.ds(*groups[group])
        slot = number * LINE + step
        block = block_of(lax.rem(line + step, LINE), lax.rem(row + number, rows), core, rows)
        core_copies[group, slot].wait_recv()
        return partial[block, chosen].astype(wide) + from_core[slot, chosen].astype(wide)

    def sum_rows(group):
        chosen = pl.ds(*groups[group])
        for number in range(1, rows):
            for step in order:
                slot = number * LINE + step
                to_row[slot, chosen] = of_chip(group, number, step).astype(narrow)
                row_copies[group, slot] = remote(
                    to_row.at[slot, chosen],
                    from_row.at[slot, chosen],
                    row_send.at[group, slot],
                    row_recv.at[group, slot],
                    across[number - 1],
                )

    def of_rows(group, step):
        value = of_chip(group, 0, step)
        for number in range(1, rows):
            slot = number * LINE + step
            row_copies[group, slot].wait_recv()
            value = value + from_row[slot, pl.ds(*groups[group])].astype(wide)
        return value

    def sum_line(group):
        chosen = pl.ds(*groups[group])
        for step in range(1, LINE):
            to_line[step, chosen] = of_rows(group, step).astype(narrow)
            line_copies[group, step] = remote(
                to_line.at[step, chosen],
                from_line.at[step, chosen],
                line_send.at[group, step],
                line_recv.at[group, step],
                along[step - 1],
            )

    def sum_last(group):
        chosen = pl.ds(*groups[group])
        value = of_rows(group, 0)
        for step in range(1, LINE):
            line_copies[group, step].wait_recv()
            value = value + from_line[step, chosen].astype(wide)
        out_ref[tm, chosen] = value.astype(narrow)
        view = out_ref.at[tm, chosen]
        last_copies.append(
            remote(view, view, last_send.at[group], last_recv.at[group], partner)
        )

    def store(number, value):
        partial[:, number] = value.astype(narrow).reshape(
            partial.shape[0], partial.shape[2], half
        )

    def lay_out():
        for frame in range(frames):
            value = u_all[frame // own, frame % own].astype(wide)
            fill_columns(
                columns, width + frame * stride, value / (1.0 + jnp.exp(-value)), width, False
            )
        columns_t[...] = columns[...].T

    def lay_out_grads():
        for frame in range(frames):
            place = slice((frame + 1) * pixels, (frame + 2) * pixels)
            even_ref[place] = c_all[frame // own, frame % own, 0]
            odd_ref[place] = c_all[frame // own, frame % own, 1]

    def temporal_back():
        even = even_ref[pixels : (frames + 1) * pixels]
        odd = odd_ref[pixels : (frames + 1) * pixels]
        here = contract_cols(even, tap(2)) + contract_cols(odd, tap(2))
        here = here + contract_cols(odd, tap(1))
        ahead = contract_cols(even, tap(0)) + contract_cols(odd, tap(0))
        ahead = ahead + contract_cols(even, tap(1))
        for frame in range(frames):
            value = here[frame * pixels : (frame + 1) * pixels]
            if frame == 0:
                value = value + ahead[:pixels]
            if frame < frames - 1:
                value = value + ahead[(frame + 1) * pixels : (frame + 2) * pixels]
            place = 2 * width + frame * stride
            g_ref[place : place + pixels] = value.astype(narrow)

    def spatial_weight_grads():
        depth = columns.shape[0]
        for r in range(3):
            begin = (2 - r) * width
            value = wide_dot(columns_t[...], g_ref[begin : begin + depth, lanes])
            for s in range(3):
                store(3 + 3 * r + s, value[s * channels : (s + 1) * channels])

    def spatial_row(r):
        value = wide_dot(
            columns[r * width : r * width + span],
            ws_all[3 * r : 3 * r + 3].reshape(3 * channels, half),
        )
        total_ref[...] = value if r == 0 else total_ref[...] + value

    def spatial_done():
        for frame in range(frames):
            value = total_ref[frame * stride : frame * stride + pixels].astype(narrow)
            s_halves[tm, frame * pixels : (frame + 1) * pixels] = value
        view = s_halves.at[tm]
        pairs.append(remote(view, view, pair_send.at[2], pair_recv.at[2], partner))

    def spatial_join():
        pairs[2].wait_recv()
        for side in range(2):
            columns_of = slice(side * half, (side + 1) * half)
            s_ref[pixels : (frames + 1) * pixels, columns_of] = s_halves[side]
            s_ref[:pixels, columns_of] = s_halves[side, :pixels]

    def temporal_weight_grads():
        s_t[...] = s_ref[...].T
        extent = s_ref.shape[0]
        past_even = wide_dot(s_t[...], even_ref[pixels : pixels + extent, lanes])
        now_odd = wide_dot(s_t[...], odd_ref[:extent, lanes])
        store(1, past_even + now_odd)
        store(0, past_even + wide_dot(s_t[...], odd_ref[pixels : pixels + extent, lanes]))
        store(2, now_odd + wide_dot(s_t[...], even_ref[:extent, lanes]))

    def decode():
        start = tm * (own * pixels)
        past = s_ref[pl.ds(pl.multiple_of(start, 16), own * pixels)]
        now = s_ref[pl.ds(pl.multiple_of(start + pixels, 16), own * pixels)]
        base = wide_dot(past, tap(0)) + wide_dot(now, tap(2))
        first = base + wide_dot(past, tap(1))
        second = base + wide_dot(now, tap(1))
        for frame in range(own):
            place = slice(frame * pixels, (frame + 1) * pixels)
            value = u_all[tm, frame].astype(wide)
            decoded_ref[frame, 0] = (value + first[place]).astype(narrow)
            decoded_ref[frame, 1] = (value + second[place]).astype(narrow)

    def rows_of(side, frame):
        return pl.ds(pl.multiple_of((side * own + frame) * stride, 16), pixels)

    def spatial_back():
        for frame in range(frames):
            place = 2 * width + frame * stride
            flat = g_ref[place : place + pixels, lanes].astype(wide)
            fill_columns(spread, width + frame * stride, flat, width, True)
        value = jnp.zeros((span, channels), wide)
        for r in range(3):
            begin = (2 - r) * width
            for s in range(3):
                value = value + contract_cols(
                    spread[begin : begin + span, s * half : (s + 1) * half],
                    ws_all[3 * r + s].reshape(channels, half),
                )
        act_total[...] = value
        for frame in range(own):
            act_out[frame] = act_total[rows_of(1 - tm, frame)].astype(narrow)
        pairs.append(remote(act_out, act_in, pair_send.at[3], pair_recv.at[3], partner))

    def input_grads():
        pairs[3].wait_recv()
        for frame in range(own):
            part = act_total[rows_of(tm, frame)] + act_in[frame].astype(wide)
            held = u_all[tm, frame].astype(wide)
            sigmoid = 1.0 / (1.0 + jnp.exp(-held))
            slope = sigmoid * (1.0 + held * (1.0 - sigmoid))
            pair = c_all[tm, frame, 0].astype(wide) + c_all[tm, frame, 1].astype(wide)
            input_ref[frame] = (pair + part * slope).astype(narrow)

    push_own(0)
    pairs = [
        remote(u_ref, u_all.at[tm], pair_send.at[0], pair_recv.at[0], partner),
        remote(c_ref, c_all.at[tm], pair_send.at[1], pair_recv.at[1], partner),
    ]
    for part in range(1, PARTS):
        push_own(part)
    kept = [
        pltpu.make_async_copy(wt_ref, wt_all.at[:, me], own_sem.at[0]),
        pltpu.make_async_copy(ws_ref.at[:, :, lanes], ws_all.at[:, me], own_sem.at[3]),
        pltpu.make_async_copy(u_ref, u_all.at[tm], own_sem.at[1]),
        pltpu.make_async_copy(c_ref, c_all.at[tm], own_sem.at[2]),
    ]
    for copy in kept:
        copy.start()
    for scratch in (columns, s_ref, g_ref, even_ref, odd_ref, spread):
        scratch[...] = jnp.zeros_like(scratch)
    relay_line(0)
    relay_line(1)
    relay_rows(0)
    for copy in kept:
        copy.wait()
    pairs[0].wait_recv()
    lay_out()
    pairs[1].wait_recv()
    lay_out_grads()
    relay_line(2)
    complete(0)
    temporal_back()
    relay_rows(1)
    relay_line(3)
    spatial_weight_grads()
    sum_core(0)
    relay_rows(2)
    sum_rows(0)
    complete(1)
    spatial_row(0)
    relay_rows(3)
    complete(2)
    spatial_row(1)
    complete(3)
    spatial_row(2)
    spatial_done()
    spatial_back()
    sum_line(0)
    spatial_join()
    temporal_weight_grads()
    sum_core(1)
    sum_rows(1)
    decode()
    sum_line(1)
    input_grads()
    sum_last(0)
    sum_last(1)
    for copy in sent + pairs:
        copy.wait_send()
    for copies in (core_copies, row_copies, line_copies):
        for copy in copies.values():
            copy.wait_send()
    for copy in last_copies:
        copy.wait()
    for side in range(2):
        gt_ref[:, :, side * half : (side + 1) * half] = out_ref[side, :taps]
        gs_ref[:, :, side * half : (side + 1) * half] = out_ref[side, taps:]


def section(w_temporal, w_spatial, source, upstream, width, devices):
    rows = devices // (2 * LINE)
    own, pixels, channels = source.shape
    block = w_temporal.shape[1]
    taps = w_temporal.shape[0] + w_spatial.shape[0]
    frames, half = 2 * own, channels // 2
    stride = pixels + width
    depth = up_to(width + frames * stride, 256)
    extent = up_to((frames + 1) * pixels, 128)
    many = rows * LINE
    slots = (LINE - 1) + LINE * (rows - 1) + many
    kept = source.dtype
    anywhere = pl.BlockSpec(memory_space=pl.ANY)
    in_vmem = pl.BlockSpec(memory_space=pltpu.VMEM)
    dma = pltpu.SemaphoreType.DMA
    return pl.pallas_call(
        functools.partial(section_kernel, rows, width),
        out_shape=(
            jax.ShapeDtypeStruct((own, 2, pixels, channels), kept),
            jax.ShapeDtypeStruct((own, pixels, channels), kept),
            jax.ShapeDtypeStruct(w_spatial.shape, kept),
            jax.ShapeDtypeStruct(w_temporal.shape, kept),
        ),
        in_specs=[anywhere] * 4,
        out_specs=(in_vmem,) * 4,
        scratch_shapes=[
            pltpu.VMEM((2, taps, block, half), kept),
            pltpu.VMEM((w_temporal.shape[0], devices, block, channels), kept),
            pltpu.VMEM((w_spatial.shape[0], devices, block, half), kept),
            pltpu.VMEM((2, own, pixels, channels), kept),
            pltpu.VMEM((2, own, 2, pixels, channels), kept),
            pltpu.VMEM((devices, taps, block, half), kept),
            pltpu.VMEM((depth, 3 * channels), kept),
            pltpu.VMEM((3 * channels, depth), kept),
            pltpu.VMEM((extent, channels), kept),
            pltpu.VMEM((channels, extent), kept),
            pltpu.VMEM((depth + 2 * width, channels), kept),
            pltpu.VMEM((extent + pixels, channels), kept),
            pltpu.VMEM((extent + pixels, channels), kept),
            pltpu.VMEM((width + frames * stride, 3 * half), kept),
            pltpu.VMEM((frames * stride - width, half), jnp.float32),
            pltpu.VMEM((2, frames * pixels, half), kept),
            pltpu.VMEM((frames * stride - width, channels), jnp.float32),
            pltpu.VMEM((own, pixels, channels), kept),
            pltpu.VMEM((own, pixels, channels), kept),
            pltpu.VMEM((many, taps, block, half), kept),
            pltpu.VMEM((many, taps, block, half), kept),
            pltpu.VMEM((many, taps, block, half), kept),
            pltpu.VMEM((LINE, taps, block, half), kept),
            pltpu.VMEM((LINE, taps, block, half), kept),
            dma((PARTS, slots)),
            dma((PARTS, devices)),
            dma((4,)),
            dma((4,)),
            dma((4,)),
            dma((2, many)),
            dma((2, many)),
            dma((2, many)),
            dma((2, many)),
            dma((2, LINE)),
            dma((2, LINE)),
            dma((2,)),
            dma((2,)),
        ],
        compiler_params=pltpu.CompilerParams(
            collective_id=0, has_side_effects=True, vmem_limit_bytes=58 * 2**20
        ),
        cost_estimate=pl.CostEstimate(
            flops=20 * frames * pixels * channels * channels * 2,
            bytes_accessed=12 * 2**20,
            transcendentals=2 * frames * pixels * channels,
        ),
        name="section",
    )(w_temporal, w_spatial, source, upstream)


def paired_device(frames_in, cotangent, w_spatial, w_temporal):
    devices = lax.axis_size("dp")
    source = frames_in[0]
    own, height, width, channels = source.shape
    frames, pixels = 2 * own, height * width
    decoded, grad_input, grad_s, grad_t = section(
        w_temporal,
        w_spatial,
        source.reshape(own, pixels, channels),
        cotangent[0].reshape(own, 2, pixels, channels),
        width,
        devices,
    )
    inverse = 1.0 / math.sqrt(devices * 2 * frames * pixels)
    return (
        decoded.reshape(1, 2 * own, height, width, channels),
        grad_input.reshape(1, own, height, width, channels),
        grad_s.astype(jnp.float32) * inverse,
        grad_t.astype(jnp.float32) * inverse,
    )


def solution(mesh):
    clip_split = P("dp", "tm", None, None, None)
    rows_split = P(None, "dp", None)
    paired = mesh.shape["tm"] == 2 and mesh.shape["dp"] % (2 * LINE) == 0
    return jax.shard_map(
        paired_device if paired else per_device,
        mesh=mesh,
        in_specs=(clip_split, clip_split, rows_split, rows_split),
        out_specs=(clip_split, clip_split, rows_split, rows_split),
        check_vma=False,
    )
```

```python
import functools
import math

import jax
import jax.numpy as jnp
from jax import lax
from jax.experimental import pallas as pl
from jax.experimental.pallas import tpu as pltpu
from jax.sharding import PartitionSpec as P

MESH = pl.DeviceIdType.MESH
LINE = 4
PARTS = 4

spatial_taps = [(row_shift, col_shift) for row_shift in range(3) for col_shift in range(3)]


def passed_along(value, axis, steps):
    count = lax.axis_size(axis)
    leading, last = (max(0, -steps), min(count, count - steps))
    return lax.ppermute(value, axis, [(source, source + steps) for source in range(leading, last)])


def contract_rows(left, right):
    return lax.dot_general(
        left, right, (((0,), (0,)), ((), ())), preferred_element_type=jnp.float32
    )


def contract_cols(left, right):
    return lax.dot_general(
        left, right, (((1,), (1,)), ((), ())), preferred_element_type=jnp.float32
    )


def silu_slope(value):
    sigmoid = jax.nn.sigmoid(value)
    return sigmoid * (1.0 + value * (1.0 - sigmoid))


def spatial_forward(padded_act, weight):
    height = padded_act.shape[1] - 2
    width = padded_act.shape[2] - 2
    total = jnp.float32(0.0)
    for position, (row_shift, col_shift) in enumerate(spatial_taps):
        window = padded_act[
            :, row_shift : row_shift + height, col_shift : col_shift + width
        ].reshape(-1, padded_act.shape[3])
        total = total + jnp.dot(window, weight[position], preferred_element_type=jnp.float32)
    return total


def spatial_transpose(grad_flat, weight, frames, height, width):
    result = jnp.zeros((frames, height + 2, width + 2, weight.shape[1]), jnp.float32)
    for position, (row_shift, col_shift) in enumerate(spatial_taps):
        part = contract_cols(grad_flat, weight[position]).reshape(
            frames, height, width, weight.shape[1]
        )
        result = result.at[:, row_shift : row_shift + height, col_shift : col_shift + width].add(
            part
        )
    return result[:, 1:-1, 1:-1]


def temporal_forward(stacked, weight, frames):
    total = jnp.float32(0.0)
    for lag_step in range(3):
        window = stacked[lag_step : lag_step + frames].reshape(-1, stacked.shape[3])
        total = total + jnp.dot(window, weight[lag_step], preferred_element_type=jnp.float32)
    return total


def temporal_transpose(grad_flat, weight, frames, height, width):
    total = jnp.zeros((frames + 2, height, width, weight.shape[1]), jnp.float32)
    for lag_step in range(3):
        part = contract_cols(grad_flat, weight[lag_step]).reshape(
            frames, height, width, weight.shape[1]
        )
        total = total + jnp.pad(part, ((lag_step, 2 - lag_step), (0, 0), (0, 0), (0, 0)))
    return total


def weight_grads(padded_act, stacked, grad_frames, upstream_frames, frames, height, width):
    columns = grad_frames.shape[-1]
    channels = padded_act.shape[-1]
    upstream_flat = upstream_frames.reshape(-1, columns)
    grad_t = jnp.stack(
        [
            contract_rows(
                stacked[lag_step : lag_step + frames].reshape(-1, channels), upstream_flat
            )
            for lag_step in range(3)
        ]
    )
    collected = []
    for row_shift, col_shift in spatial_taps:
        window = padded_act[
            :, row_shift : row_shift + height, col_shift : col_shift + width
        ].reshape(-1, channels)
        collected.append(contract_rows(window, grad_frames))
    return (jnp.stack(collected), grad_t)


def per_device(frames_in, cotangent, w_spatial, w_temporal):
    source = frames_in[0]
    upstream = cotangent[0]
    frames = 2 * source.shape[0]
    height, width, channels = (source.shape[1], source.shape[2], source.shape[3])
    voxels = frames * height * width
    first_device = lax.axis_index("tm") == 0
    upsampled = jnp.repeat(source, 2, axis=0)
    up_float = upsampled.astype(jnp.float32)
    activated = jax.nn.silu(up_float).astype(jnp.bfloat16)
    padded_act = jnp.pad(activated, ((0, 0), (1, 1), (1, 1), (0, 0)))
    columns = padded_act
    spatial_sum = spatial_forward(columns, lax.all_gather(w_spatial, "dp", axis=1, tiled=True))
    spatial_out = spatial_sum.reshape(frames, height, width, channels).astype(jnp.bfloat16)
    previous = passed_along(spatial_out[frames - 2 :], "tm", 1)
    previous = jnp.where(first_device, jnp.broadcast_to(spatial_out[:1], previous.shape), previous)
    stacked = jnp.concatenate([previous, spatial_out], axis=0)
    columns = stacked
    temporal_sum = temporal_forward(
        columns, lax.all_gather(w_temporal, "dp", axis=1, tiled=True), frames
    )
    decoded = (up_float + temporal_sum.reshape(frames, height, width, channels)).astype(
        jnp.bfloat16
    )
    following = passed_along(upstream[:2], "tm", -1)
    extended_flat = jnp.concatenate([upstream, following], axis=0).reshape(-1, channels)
    piece = lax.all_gather(w_temporal, "dp", axis=1, tiled=True)
    pad_grad = temporal_transpose(extended_flat, piece, frames + 2, height, width)
    inner = pad_grad[2 : frames + 2]
    edge = jnp.where(first_device, pad_grad[0] + pad_grad[1], jnp.zeros_like(pad_grad[0]))
    inner = inner.at[0].add(edge)
    inner_grad = inner.reshape(voxels, piece.shape[1])
    spatial_grad = inner_grad.astype(jnp.bfloat16)
    grad_s_local, grad_t_local = weight_grads(
        padded_act, stacked, spatial_grad, upstream, frames, height, width
    )
    owned_s, owned_t = (
        lax.psum_scatter(grad_s_local, "dp", scatter_dimension=1, tiled=True),
        lax.psum_scatter(grad_t_local, "dp", scatter_dimension=1, tiled=True),
    )
    summed_s, summed_t = lax.psum((owned_s, owned_t), "tm")
    piece = lax.all_gather(w_spatial, "dp", axis=1, tiled=True)
    act_flat = spatial_transpose(spatial_grad, piece, frames, height, width).reshape(
        voxels, piece.shape[1]
    )
    act_grad = act_flat.reshape(frames, height, width, channels)
    up_grad = upstream.astype(jnp.float32) + act_grad * silu_slope(up_float)
    grad_input = (
        up_grad.reshape(frames // 2, 2, height, width, channels).sum(axis=1).astype(jnp.bfloat16)
    )
    inverse = 1.0 / math.sqrt(lax.axis_size("dp") * lax.axis_size("tm") * voxels)
    return (decoded[None], grad_input[None], summed_s * inverse, summed_t * inverse)


def places(line, rows):
    index = lax.axis_index("dp")
    core = lax.rem(index, 2)
    row = lax.rem(index // 2, rows)
    return index // (2 * rows), row, core, lax.axis_index("tm")


def block_of(line, row, core, rows):
    return (line * rows + row) * 2 + core


def greet(peers):
    barrier = pltpu.get_barrier_semaphore()
    for peer in peers:
        pl.semaphore_signal(barrier, inc=1, device_id=peer, device_id_type=MESH)
    pl.semaphore_wait(barrier, len(peers))


def peers_of(line, row, core, tm, rows):
    along = [
        (block_of(lax.rem(line + step, LINE), row, core, rows), tm) for step in range(1, LINE)
    ]
    across = [
        (block_of(line, lax.rem(row + step, rows), core, rows), tm) for step in range(1, rows)
    ]
    sibling = (block_of(line, row, 1 - core, rows), tm)
    partner = (block_of(line, row, core, rows), 1 - tm)
    return along, across, sibling, partner


def wide_dot(left, right):
    return jnp.dot(left, right, preferred_element_type=jnp.float32)


def column_shifts(flat, width):
    count = flat.shape[0]
    column = lax.rem(lax.broadcasted_iota(jnp.int32, flat.shape, 0), width)
    left = jnp.where(column == 0, 0.0, pltpu.roll(flat, 1, 0))
    right = jnp.where(column == width - 1, 0.0, pltpu.roll(flat, count - 1, 0))
    return left, flat, right


def fill_columns(target, place, flat, width, flip):
    channels = flat.shape[1]
    shifts = column_shifts(flat, width)
    for number, value in enumerate(shifts[::-1] if flip else shifts):
        target[place : place + flat.shape[0], number * channels : (number + 1) * channels] = (
            value.astype(jnp.bfloat16)
        )


def up_to(count, step):
    return -(-count // step) * step


def section_kernel(
    rows,
    width,
    wt_ref,
    ws_ref,
    u_ref,
    c_ref,
    decoded_ref,
    input_ref,
    gs_ref,
    gt_ref,
    out_ref,
    wt_all,
    ws_all,
    u_all,
    c_all,
    partial,
    columns,
    columns_t,
    s_ref,
    s_t,
    g_ref,
    even_ref,
    odd_ref,
    spread,
    total_ref,
    s_halves,
    act_total,
    act_out,
    act_in,
    from_core,
    to_row,
    from_row,
    to_line,
    from_line,
    send_sem,
    recv_sem,
    pair_send,
    pair_recv,
    own_sem,
    core_send,
    core_recv,
    row_send,
    row_recv,
    line_send,
    line_recv,
    last_send,
    last_recv,
):
    line, row, core, tm = places(LINE, rows)
    along, across, sibling, partner = peers_of(line, row, core, tm, rows)
    greet(along + across + [sibling, partner])
    taps = wt_ref.shape[0]
    me = block_of(line, row, core, rows)
    own, _, pixels, channels = c_ref.shape
    frames = 2 * own
    stride = pixels + width
    span = frames * stride - width
    half = partial.shape[3]
    lanes = pl.ds(pl.multiple_of(tm * half, half), half)
    wide = jnp.float32
    narrow = jnp.bfloat16
    sent = []

    def remote(source, target, send, recv, peer):
        copy = pltpu.make_async_remote_copy(
            src_ref=source,
            dst_ref=target,
            send_sem=send,
            recv_sem=recv,
            device_id=peer,
            device_id_type=MESH,
        )
        copy.start()
        return copy

    def place_of(part, block):
        if part == 0:
            return wt_all.at[:, block]
        return ws_all.at[pl.ds((part - 1) * taps, taps), block]

    def push(part, source, block, peer, slot):
        sent.append(
            remote(source, place_of(part, block), send_sem.at[part, slot], recv_sem.at[part, block], peer)
        )

    def landed(part, block):
        view = place_of(part, block)
        pltpu.make_async_copy(view, view, recv_sem.at[part, block]).wait()
        return view

    first_across = LINE - 1
    first_core = first_across + LINE * (rows - 1)

    def push_own(part):
        block = wt_ref if part == 0 else ws_ref.at[pl.ds((part - 1) * taps, taps), :, lanes]
        for step, peer in enumerate(along):
            push(part, block, me, peer, step)
        for step, peer in enumerate(across):
            push(part, block, me, peer, first_across + step)
        push(part, block, me, sibling, first_core)

    def relay_line(part):
        for step in range(1, LINE):
            block = block_of(lax.rem(line + step, LINE), row, core, rows)
            view = landed(part, block)
            for number, peer in enumerate(across):
                push(part, view, block, peer, first_across + step * (rows - 1) + number)
            push(part, view, block, sibling, first_core + step)

    def relay_rows(part):
        for number in range(1, rows):
            for step in range(LINE):
                block = block_of(
                    lax.rem(line + step, LINE), lax.rem(row + number, rows), core, rows
                )
                push(part, landed(part, block), block, sibling, first_core + number * LINE + step)

    def complete(part):
        for number in range(rows):
            for step in range(LINE):
                landed(part, block_of(step, number, 1 - core, rows))

    def tap(number):
        return wt_all[number].reshape(channels, channels)

    order = list(range(1, LINE)) + [0]
    core_copies, row_copies, line_copies, last_copies = {}, {}, {}, []
    groups = ((3, 9), (0, 3))

    def sum_core(group):
        chosen = pl.ds(*groups[group])
        for number in list(range(1, rows)) + [0]:
            for step in order:
                slot = number * LINE + step
                block = block_of(
                    lax.rem(line + step, LINE), lax.rem(row + number, rows), 1 - core, rows
                )
                core_copies[group, slot] = remote(
                    partial.at[block, chosen],
                    from_core.at[slot, chosen],
                    core_send.at[group, slot],
                    core_recv.at[group, slot],
                    sibling,
                )

    def of_chip(group, number, step):
        chosen = pl.ds(*groups[group])
        slot = number * LINE + step
        block = block_of(lax.rem(line + step, LINE), lax.rem(row + number, rows), core, rows)
        core_copies[group, slot].wait_recv()
        return partial[block, chosen].astype(wide) + from_core[slot, chosen].astype(wide)

    def sum_rows(group):
        chosen = pl.ds(*groups[group])
        for number in range(1, rows):
            for step in order:
                slot = number * LINE + step
                to_row[slot, chosen] = of_chip(group, number, step).astype(narrow)
                row_copies[group, slot] = remote(
                    to_row.at[slot, chosen],
                    from_row.at[slot, chosen],
                    row_send.at[group, slot],
                    row_recv.at[group, slot],
                    across[number - 1],
                )

    def of_rows(group, step):
        value = of_chip(group, 0, step)
        for number in range(1, rows):
            slot = number * LINE + step
            row_copies[group, slot].wait_recv()
            value = value + from_row[slot, pl.ds(*groups[group])].astype(wide)
        return value

    def sum_line(group):
        chosen = pl.ds(*groups[group])
        for step in range(1, LINE):
            to_line[step, chosen] = of_rows(group, step).astype(narrow)
            line_copies[group, step] = remote(
                to_line.at[step, chosen],
                from_line.at[step, chosen],
                line_send.at[group, step],
                line_recv.at[group, step],
                along[step - 1],
            )

    def sum_last(group):
        chosen = pl.ds(*groups[group])
        value = of_rows(group, 0)
        for step in range(1, LINE):
            line_copies[group, step].wait_recv()
            value = value + from_line[step, chosen].astype(wide)
        out_ref[tm, chosen] = value.astype(narrow)
        view = out_ref.at[tm, chosen]
        last_copies.append(
            remote(view, view, last_send.at[group], last_recv.at[group], partner)
        )

    def store(number, value):
        partial[:, number] = value.astype(narrow).reshape(
            partial.shape[0], partial.shape[2], half
        )

    def lay_out():
        for frame in range(frames):
            value = u_all[frame // own, frame % own].astype(wide)
            fill_columns(
                columns, width + frame * stride, value / (1.0 + jnp.exp(-value)), width, False
            )
        columns_t[...] = columns[...].T

    def lay_out_grads():
        for frame in range(frames):
            place = slice((frame + 1) * pixels, (frame + 2) * pixels)
            even_ref[place] = c_all[frame // own, frame % own, 0]
            odd_ref[place] = c_all[frame // own, frame % own, 1]

    def temporal_back():
        even = even_ref[pixels : (frames + 1) * pixels]
        odd = odd_ref[pixels : (frames + 1) * pixels]
        here = contract_cols(even, tap(2)) + contract_cols(odd, tap(2))
        here = here + contract_cols(odd, tap(1))
        ahead = contract_cols(even, tap(0)) + contract_cols(odd, tap(0))
        ahead = ahead + contract_cols(even, tap(1))
        for frame in range(frames):
            value = here[frame * pixels : (frame + 1) * pixels]
            if frame == 0:
                value = value + ahead[:pixels]
            if frame < frames - 1:
                value = value + ahead[(frame + 1) * pixels : (frame + 2) * pixels]
            place = 2 * width + frame * stride
            g_ref[place : place + pixels] = value.astype(narrow)

    def spatial_weight_grads():
        depth = columns.shape[0]
        for r in range(3):
            begin = (2 - r) * width
            value = wide_dot(columns_t[...], g_ref[begin : begin + depth, lanes])
            for s in range(3):
                store(3 + 3 * r + s, value[s * channels : (s + 1) * channels])

    def spatial_row(r):
        value = wide_dot(
            columns[r * width : r * width + span],
            ws_all[3 * r : 3 * r + 3].reshape(3 * channels, half),
        )
        total_ref[...] = value if r == 0 else total_ref[...] + value

    def spatial_done():
        for frame in range(frames):
            value = total_ref[frame * stride : frame * stride + pixels].astype(narrow)
            s_halves[tm, frame * pixels : (frame + 1) * pixels] = value
        view = s_halves.at[tm]
        pairs.append(remote(view, view, pair_send.at[2], pair_recv.at[2], partner))

    def spatial_join():
        pairs[2].wait_recv()
        for side in range(2):
            columns_of = slice(side * half, (side + 1) * half)
            s_ref[pixels : (frames + 1) * pixels, columns_of] = s_halves[side]
            s_ref[:pixels, columns_of] = s_halves[side, :pixels]

    def temporal_weight_grads():
        s_t[...] = s_ref[...].T
        extent = s_ref.shape[0]
        past_even = wide_dot(s_t[...], even_ref[pixels : pixels + extent, lanes])
        now_odd = wide_dot(s_t[...], odd_ref[:extent, lanes])
        store(1, past_even + now_odd)
        store(0, past_even + wide_dot(s_t[...], odd_ref[pixels : pixels + extent, lanes]))
        store(2, now_odd + wide_dot(s_t[...], even_ref[:extent, lanes]))

    def decode():
        start = tm * (own * pixels)
        past = s_ref[pl.ds(pl.multiple_of(start, 16), own * pixels)]
        now = s_ref[pl.ds(pl.multiple_of(start + pixels, 16), own * pixels)]
        base = wide_dot(past, tap(0)) + wide_dot(now, tap(2))
        first = base + wide_dot(past, tap(1))
        second = base + wide_dot(now, tap(1))
        for frame in range(own):
            place = slice(frame * pixels, (frame + 1) * pixels)
            value = u_all[tm, frame].astype(wide)
            decoded_ref[frame, 0] = (value + first[place]).astype(narrow)
            decoded_ref[frame, 1] = (value + second[place]).astype(narrow)

    def rows_of(side, frame):
        return pl.ds(pl.multiple_of((side * own + frame) * stride, 16), pixels)

    def spatial_back():
        for frame in range(frames):
            place = 2 * width + frame * stride
            flat = g_ref[place : place + pixels, lanes].astype(wide)
            fill_columns(spread, width + frame * stride, flat, width, True)
        value = jnp.zeros((span, channels), wide)
        for r in range(3):
            begin = (2 - r) * width
            for s in range(3):
                value = value + contract_cols(
                    spread[begin : begin + span, s * half : (s + 1) * half],
                    ws_all[3 * r + s].reshape(channels, half),
                )
        act_total[...] = value
        for frame in range(own):
            act_out[frame] = act_total[rows_of(1 - tm, frame)].astype(narrow)
        pairs.append(remote(act_out, act_in, pair_send.at[3], pair_recv.at[3], partner))

    def input_grads():
        pairs[3].wait_recv()
        for frame in range(own):
            part = act_total[rows_of(tm, frame)] + act_in[frame].astype(wide)
            held = u_all[tm, frame].astype(wide)
            sigmoid = 1.0 / (1.0 + jnp.exp(-held))
            slope = sigmoid * (1.0 + held * (1.0 - sigmoid))
            pair = c_all[tm, frame, 0].astype(wide) + c_all[tm, frame, 1].astype(wide)
            input_ref[frame] = (pair + part * slope).astype(narrow)

    push_own(0)
    pairs = [
        remote(u_ref, u_all.at[tm], pair_send.at[0], pair_recv.at[0], partner),
        remote(c_ref, c_all.at[tm], pair_send.at[1], pair_recv.at[1], partner),
    ]
    for part in range(1, PARTS):
        push_own(part)
    kept = [
        pltpu.make_async_copy(wt_ref, wt_all.at[:, me], own_sem.at[0]),
        pltpu.make_async_copy(ws_ref.at[:, :, lanes], ws_all.at[:, me], own_sem.at[3]),
        pltpu.make_async_copy(u_ref, u_all.at[tm], own_sem.at[1]),
        pltpu.make_async_copy(c_ref, c_all.at[tm], own_sem.at[2]),
    ]
    for copy in kept:
        copy.start()
    for scratch in (columns, s_ref, g_ref, even_ref, odd_ref, spread):
        scratch[...] = jnp.zeros_like(scratch)
    relay_line(0)
    relay_line(1)
    relay_rows(0)
    for copy in kept:
        copy.wait()
    pairs[0].wait_recv()
    lay_out()
    pairs[1].wait_recv()
    lay_out_grads()
    complete(0)
    temporal_back()
    relay_line(2)
    spatial_weight_grads()
    sum_core(0)
    relay_rows(1)
    relay_line(3)
    sum_rows(0)
    relay_rows(2)
    complete(1)
    spatial_row(0)
    relay_rows(3)
    complete(2)
    spatial_row(1)
    complete(3)
    spatial_row(2)
    spatial_done()
    spatial_back()
    sum_line(0)
    spatial_join()
    temporal_weight_grads()
    sum_core(1)
    sum_rows(1)
    decode()
    sum_line(1)
    input_grads()
    sum_last(0)
    sum_last(1)
    for copy in sent + pairs:
        copy.wait_send()
    for copies in (core_copies, row_copies, line_copies):
        for copy in copies.values():
            copy.wait_send()
    for copy in last_copies:
        copy.wait()
    for side in range(2):
        gt_ref[:, :, side * half : (side + 1) * half] = out_ref[side, :taps]
        gs_ref[:, :, side * half : (side + 1) * half] = out_ref[side, taps:]


def section(w_temporal, w_spatial, source, upstream, width, devices):
    rows = devices // (2 * LINE)
    own, pixels, channels = source.shape
    block = w_temporal.shape[1]
    taps = w_temporal.shape[0] + w_spatial.shape[0]
    frames, half = 2 * own, channels // 2
    stride = pixels + width
    depth = up_to(width + frames * stride, 256)
    extent = up_to((frames + 1) * pixels, 128)
    many = rows * LINE
    slots = (LINE - 1) + LINE * (rows - 1) + many
    kept = source.dtype
    anywhere = pl.BlockSpec(memory_space=pl.ANY)
    in_vmem = pl.BlockSpec(memory_space=pltpu.VMEM)
    dma = pltpu.SemaphoreType.DMA
    return pl.pallas_call(
        functools.partial(section_kernel, rows, width),
        out_shape=(
            jax.ShapeDtypeStruct((own, 2, pixels, channels), kept),
            jax.ShapeDtypeStruct((own, pixels, channels), kept),
            jax.ShapeDtypeStruct(w_spatial.shape, kept),
            jax.ShapeDtypeStruct(w_temporal.shape, kept),
        ),
        in_specs=[anywhere] * 4,
        out_specs=(in_vmem,) * 4,
        scratch_shapes=[
            pltpu.VMEM((2, taps, block, half), kept),
            pltpu.VMEM((w_temporal.shape[0], devices, block, channels), kept),
            pltpu.VMEM((w_spatial.shape[0], devices, block, half), kept),
            pltpu.VMEM((2, own, pixels, channels), kept),
            pltpu.VMEM((2, own, 2, pixels, channels), kept),
            pltpu.VMEM((devices, taps, block, half), kept),
            pltpu.VMEM((depth, 3 * channels), kept),
            pltpu.VMEM((3 * channels, depth), kept),
            pltpu.VMEM((extent, channels), kept),
            pltpu.VMEM((channels, extent), kept),
            pltpu.VMEM((depth + 2 * width, channels), kept),
            pltpu.VMEM((extent + pixels, channels), kept),
            pltpu.VMEM((extent + pixels, channels), kept),
            pltpu.VMEM((width + frames * stride, 3 * half), kept),
            pltpu.VMEM((frames * stride - width, half), jnp.float32),
            pltpu.VMEM((2, frames * pixels, half), kept),
            pltpu.VMEM((frames * stride - width, channels), jnp.float32),
            pltpu.VMEM((own, pixels, channels), kept),
            pltpu.VMEM((own, pixels, channels), kept),
            pltpu.VMEM((many, taps, block, half), kept),
            pltpu.VMEM((many, taps, block, half), kept),
            pltpu.VMEM((many, taps, block, half), kept),
            pltpu.VMEM((LINE, taps, block, half), kept),
            pltpu.VMEM((LINE, taps, block, half), kept),
            dma((PARTS, slots)),
            dma((PARTS, devices)),
            dma((4,)),
            dma((4,)),
            dma((4,)),
            dma((2, many)),
            dma((2, many)),
            dma((2, many)),
            dma((2, many)),
            dma((2, LINE)),
            dma((2, LINE)),
            dma((2,)),
            dma((2,)),
        ],
        compiler_params=pltpu.CompilerParams(
            collective_id=0, has_side_effects=True, vmem_limit_bytes=58 * 2**20
        ),
        cost_estimate=pl.CostEstimate(
            flops=20 * frames * pixels * channels * channels * 2,
            bytes_accessed=12 * 2**20,
            transcendentals=2 * frames * pixels * channels,
        ),
        name="section",
    )(w_temporal, w_spatial, source, upstream)


def paired_device(frames_in, cotangent, w_spatial, w_temporal):
    devices = lax.axis_size("dp")
    source = frames_in[0]
    own, height, width, channels = source.shape
    frames, pixels = 2 * own, height * width
    decoded, grad_input, grad_s, grad_t = section(
        w_temporal,
        w_spatial,
        source.reshape(own, pixels, channels),
        cotangent[0].reshape(own, 2, pixels, channels),
        width,
        devices,
    )
    inverse = 1.0 / math.sqrt(devices * 2 * frames * pixels)
    return (
        decoded.reshape(1, 2 * own, height, width, channels),
        grad_input.reshape(1, own, height, width, channels),
        grad_s.astype(jnp.float32) * inverse,
        grad_t.astype(jnp.float32) * inverse,
    )


def solution(mesh):
    clip_split = P("dp", "tm", None, None, None)
    rows_split = P(None, "dp", None)
    paired = mesh.shape["tm"] == 2 and mesh.shape["dp"] % (2 * LINE) == 0
    return jax.shard_map(
        paired_device if paired else per_device,
        mesh=mesh,
        in_specs=(clip_split, clip_split, rows_split, rows_split),
        out_specs=(clip_split, clip_split, rows_split, rows_split),
        check_vma=False,
    )
```
